128 devices in a mesh: period: 4 (over x_hi, core), slab: 32 (over y, z, x_lo).
Axes of the slice: x: 4 (x_hi: 2, x_lo: 2; x = x_hi * 2 + x_lo), y: 4, z: 4, core: 2. Of those that a mesh axis runs over, the one named last changes fastest.
Arguments:
- final_window_dual_level: float32 [512, 16, 1024], P('slab'), may hold values from -6 to 6
- misfit: float32 [4, 512, 16, 1024], P('period', 'slab'), may hold values from -1.8 to 1.8
- conductivity: float32 [512, 16, 1024], P('slab'), may hold values from 0.3 to 3
- capacity: float32 [512, 16, 1024], P('slab'), may hold values from 0.005 to 0.05
- wells: int32 [1024], replicated, may hold values from 0 to 8388607
- plan: int32 [4, 1024], P('period'), may hold values 0 or 1
Outputs:
- corrected: float32 [4, 512, 16, 1024], P('period', 'slab')
- well_grad: float32 [1024], replicated
The draws below stay inside these ranges and needn't reach their ends.
Inputs may be any that keep to these rules, and one draw needn't show every extreme that they name: wells[w] = (x * 16 + z) * 1024 + y for the cell of well w.
All inputs are finite; a program needn't handle non-finite values. No bound on the sum of `plan` on one device may be relied on, other than what follows from the above.
Results may differ from the reference program's by a relative error of at most 0.0001.
Values sent between devices are 32-bit elements; how exact they have to be, the bound alone decides.
A program may use at most 128 MiB of HBM per device.

```python
import math
import jax
import jax.numpy as jnp

NY = 1024
NZ = 16
PER_GROUP = 1
STEPS = 2
SWEEPS = 8
CF = 16
WELLS = 1024
NX = 512
PERIODS = 4
N_PERIOD = 4


def place_ends(values, rng, low, high):
    dims = values.shape
    spot = [jax.random.randint(jax.random.fold_in(rng, axis), (), 0, dims[axis]) for axis in range(len(dims))]
    values = values.at[tuple(spot)].set(low)
    longest = dims.index(max(dims))
    spot[longest] = (spot[longest] + 1) % dims[longest]
    return values.at[tuple(spot)].set(high)


def shard_levels(stream_key, shape, split, least, largest):
    def one(dim, shards_of):
        heights = jax.random.uniform(jax.random.fold_in(jax.random.fold_in(stream_key, 6), dim), (shards_of,), jnp.float32, least / len(split), largest / len(split))
        return jnp.repeat(jnp.exp(heights), shape[dim] // shards_of).reshape((-1,) + (1,) * (len(shape) - dim - 1))

    loudness = one(*split[0])
    for cut in split[1:]:
        loudness = loudness * one(*cut)
    return loudness


def gaussian(own_key, extent, spread, most, split=(), held_as=jnp.bfloat16):
    factor_of = shard_levels(own_key, extent, split, -0.22, 0.18) if split else 1.0
    array = jax.random.normal(own_key, extent, jnp.float32) * spread * factor_of
    return jnp.minimum(jnp.maximum(array, -most), most).astype(held_as)


def setup_inputs(seed: int = 0) -> dict:
    keys = jax.random.split(jax.random.key(seed), 7)
    return {
        "final_window_dual_level": gaussian(keys[0], (NX, NZ, NY), 1.0, 6.0, ((0, 32),), jnp.float32),
        "misfit": gaussian(keys[1], (PERIODS, NX, NZ, NY), 0.3, 1.8, ((0, 4), (1, 32)), jnp.float32),
        "conductivity": jnp.clip(jnp.exp(math.log(3.0) - 2.3025851 * jax.random.uniform(keys[2], (NX, NZ, NY), jnp.float32) ** shard_levels(keys[2], (NX, NZ, NY), ((0, 32),), -0.2, 0.2)), 0.3, 3.0),
        "capacity": jnp.clip(jnp.exp(math.log(0.05) - 2.3025851 * jax.random.uniform(keys[3], (NX, NZ, NY), jnp.float32) ** shard_levels(keys[3], (NX, NZ, NY), ((0, 32),), -0.2, 0.2)), 0.005, 0.05),
        "wells": place_ends(jax.random.randint(keys[4], (WELLS,), 0, NX * NZ * NY), jax.random.fold_in(keys[4], 1), 0, (NX * NZ * NY) - 1).astype(jnp.int32),
        "plan": place_ends((jax.random.randint(keys[5], (PERIODS, WELLS), 0, 2) < 1).astype(jnp.int32), jax.random.fold_in(keys[5], 1), 0, 1),
    }


def below_y(array_in):
    return jnp.pad(array_in, ((0, 0), (0, 0), (1, 0)))[:, :, :-1]

def above_y(array_in):
    return jnp.pad(array_in, ((0, 0), (0, 0), (0, 1)))[:, :, 1:]

def below_z(array_in):
    return jnp.pad(array_in, ((0, 0), (1, 0), (0, 0)))[:, :-1, :]

def above_z(array_in):
    return jnp.pad(array_in, ((0, 0), (0, 1), (0, 0)))[:, 1:, :]

def pad_rows(array_in):
    return jnp.pad(array_in, ((1, 1), (0, 0), (0, 0)))

def face_table(widened, z_scale):
    middle = widened[1:-1]
    return (jnp.sqrt(middle * widened[:-2]), jnp.sqrt(middle * widened[2:]), jnp.sqrt(middle * below_y(middle)), jnp.sqrt(middle * above_y(middle)), z_scale * jnp.sqrt(middle * below_z(middle)), z_scale * jnp.sqrt(middle * above_z(middle)))

def inverse_diagonal(storage, transmit):
    return 1.0 / (storage + transmit[0] + transmit[1] + transmit[2] + transmit[3] + transmit[4] + transmit[5])

def relax(row_below, row_centre, row_above, source, transmit, inverse):
    nearby = transmit[0] * row_below + transmit[1] * row_above
    nearby = nearby + transmit[2] * below_y(row_centre) + transmit[3] * above_y(row_centre)
    nearby = nearby + transmit[4] * below_z(row_centre) + transmit[5] * above_z(row_centre)
    return (source + nearby) * inverse

def implicit_step(starting_level_map, source, transmit, inverse):
    current = starting_level_map
    for _ in range(SWEEPS):
        padded = pad_rows(current)
        current = relax(padded[:-2], current, padded[2:], source, transmit, inverse)
    return current

def restrict(array_in):
    height, layers, across = array_in.shape
    return array_in.reshape(height // CF, CF, layers, across // CF, CF).mean(axis=(1, 4))

def extend_level_map(coarse):
    return jnp.repeat(jnp.repeat(coarse, CF, axis=0), CF, axis=2)

def reference(final_window_dual_level, misfit, conductivity, capacity, wells, plan):
    transmit = face_table(pad_rows(conductivity), 1.0)
    inverse = inverse_diagonal(capacity, transmit)
    coarse_cond = restrict(conductivity)
    coarse_store = restrict(capacity) * (CF * CF / (STEPS * PER_GROUP))
    coarse_transmit = face_table(pad_rows(coarse_cond), float(CF * CF))
    coarse_inverse = inverse_diagonal(coarse_store, coarse_transmit)

    def rough_evolution_operator(coarse_state):
        return implicit_step(coarse_state, coarse_store * coarse_state, coarse_transmit, coarse_inverse)
    number_of_teams = N_PERIOD
    closing_solution = restrict(final_window_dual_level)
    guessed_solution = [None] * number_of_teams
    stepped_solution = [None] * number_of_teams
    for team_rank in reversed(range(number_of_teams)):
        guessed_solution[team_rank] = closing_solution if team_rank == number_of_teams - 1 else stepped_solution[team_rank + 1]
        stepped_solution[team_rank] = rough_evolution_operator(guessed_solution[team_rank])
    totals = jnp.zeros(wells.shape, jnp.float32)
    finals = []
    jump_terms = []
    for team_rank in range(number_of_teams):
        dual_piezometric_level = final_window_dual_level if team_rank == number_of_teams - 1 else extend_level_map(guessed_solution[team_rank])
        for period in reversed(range(team_rank * PER_GROUP, (team_rank + 1) * PER_GROUP)):
            for _ in range(STEPS):
                dual_piezometric_level = implicit_step(dual_piezometric_level, capacity * dual_piezometric_level + misfit[period], transmit, inverse)
                totals = totals + plan[period].astype(jnp.float32) * dual_piezometric_level.reshape(-1)[wells]
        finals.append(dual_piezometric_level)
        jump_terms.append(restrict(dual_piezometric_level) - stepped_solution[team_rank])
    carried = jnp.zeros_like(closing_solution)
    corrected = [None] * number_of_teams
    for team_rank in reversed(range(number_of_teams)):
        carry_value = jump_terms[team_rank] + rough_evolution_operator(carried)
        corrected[team_rank] = finals[team_rank] + extend_level_map(carry_value - jump_terms[team_rank])
        carried = carry_value
    return (jnp.stack(corrected), totals / (STEPS * PERIODS))
```

```python
import jax
import jax.numpy as jnp
from jax import lax
from jax.experimental import pallas as pl
from jax.experimental.pallas import tpu as pltpu
from jax.sharding import PartitionSpec as P

MESH = pl.DeviceIdType.MESH
F32 = jnp.float32
BF16 = jnp.bfloat16
STEPS = 2
SWEEPS = 8
CF = 16
X = 16
Z = 16
SLABS = 32
GROUPS = 4
W = 4
NR = X + 2 * W
NEX = STEPS * SWEEPS // W - 1
CY = 64
EXACT = lax.Precision.HIGHEST


def iota(shape, dim):
    return lax.broadcasted_iota(jnp.int32, shape, dim)


def y_below(v):
    rolled = pltpu.roll(v, 1, 2)
    return jnp.where(iota(v.shape, 2) == 0, pltpu.roll(rolled, 1, 1), rolled)


def y_above(v):
    rolled = pltpu.roll(v, 127, 2)
    return jnp.where(iota(v.shape, 2) == 127, pltpu.roll(rolled, 7, 1), rolled)


def z_below(v):
    return jnp.concatenate([v[:1], v[:-1]], 0)


def z_above(v):
    return jnp.concatenate([v[1:], v[-1:]], 0)


def cz_below(v):
    rolled = pltpu.roll(v, 1, 1)
    return jnp.where(iota(v.shape, 1) == 0, pltpu.roll(rolled, 64, 2), rolled)


def cz_above(v):
    rolled = pltpu.roll(v, 7, 1)
    return jnp.where(iota(v.shape, 1) == 7, pltpu.roll(rolled, 64, 2), rolled)


def device_of(group, row):
    return (2 * (group // 2) + row % 2, 2 * (row // 2) + group % 2)


def kernel(
    final_hbm, misfit_hbm, cond_hbm, cap_hbm, wells_ref, plan_ref,
    out_hbm, grad_ref,
    stage, condx, capx, misx, va, vb, co, inv, bi, own, rx,
    cbuf, ck, cco, cinv, cst, ga, gb, gbi, rs, pw, adv, planx, acc, sums, tot, st1, st2,
    ld_sem, ag_s, ag_r, sw_s, sw_r, id_s, id_r, hs_s, hs_r, ex_s, ex_r, e1_s, e1_r, e2_s, e2_r, own_s, own_r, out_sem,
):
    period = lax.axis_index("period")
    slab = lax.axis_index("slab")
    x_hi, core = period // 2, period % 2
    column, x_lo = slab // 2, slab % 2
    group = 2 * x_hi + x_lo
    row = 2 * column + core
    swapped = core != x_lo
    partner = (2 * x_hi + 1 - core, 2 * column + 1 - x_lo)
    far = (2 * (1 - x_hi) + core, 2 * column + 1 - x_lo)
    last = GROUPS - 1

    def load(k):
        src = (cond_hbm, cap_hbm, final_hbm, misfit_hbm)[k]
        return [
            pltpu.make_async_copy(src.at[:, :, pl.ds(128 * j, 128)], stage.at[k, :, :, j, :], ld_sem.at[k, j])
            for j in range(8)
        ]

    loads = [load(k) for k in range(4)]
    for group_of in loads:
        for copy in group_of:
            copy.start()

    barrier = pltpu.get_barrier_semaphore()

    def hello(device):
        pl.semaphore_signal(barrier, inc=1, device_id=device, device_id_type=MESH)

    def greet_slabs(k, c):
        hello((period, (slab + k) % SLABS))
        return c

    def greet_columns(k, c):
        hello((2 * x_hi + 1 - core, 2 * k + x_lo))
        return c

    lax.fori_loop(1, SLABS, greet_slabs, 0)
    lax.fori_loop(0, SLABS // 2, greet_columns, 0)
    for k in range(1, GROUPS):
        hello(device_of((group + k) % GROUPS, row))

    @pl.when(swapped)
    def _():
        hello(partner)

    fine_lane = iota((128, CY), 0)
    coarse_lane = iota((128, CY), 1)

    def restrict(block):
        rs[...] = jnp.sum(block, axis=0)
        total = jnp.zeros((Z, CY), F32)
        for s in range(8):
            pick = (coarse_lane == 8 * s + fine_lane // CF).astype(F32)
            total = total + jnp.dot(rs[:, s, :], pick, preferred_element_type=F32, precision=EXACT)
        total = total * (1.0 / (CF * CF))
        return jnp.concatenate([total[:8], total[8:]], axis=1)

    for k in range(3):
        for copy in loads[k]:
            copy.wait()
        cbuf[slab, k] = restrict(stage[k])

    pl.semaphore_wait(barrier, (SLABS - 1) + SLABS // 2 + GROUPS - 1 + swapped.astype(jnp.int32))

    def gather_copy(k, who):
        return pltpu.make_async_remote_copy(
            cbuf.at[who], cbuf.at[who], ag_s.at[k], ag_r.at[k],
            device_id=(period, (slab + k) % SLABS), device_id_type=MESH,
        )

    def gather_start(k, c):
        gather_copy(k, slab).start()
        return c

    lax.fori_loop(1, SLABS, gather_start, 0)
    for copy in loads[3]:
        copy.wait()

    body = pl.ds(W, X)

    def swap_copies(device):
        return [
            pltpu.make_async_remote_copy(
                stage.at[3], misx.at[body], sw_s.at[0], sw_r.at[0], device_id=device, device_id_type=MESH),
            pltpu.make_async_remote_copy(
                stage.at[0, pl.ds(0, 8)], condx.at[pl.ds(W + 1, 8)], sw_s.at[1], sw_r.at[1],
                device_id=device, device_id_type=MESH),
            pltpu.make_async_remote_copy(
                plan_ref, planx, sw_s.at[2], sw_r.at[2], device_id=device, device_id_type=MESH),
        ]

    def swap_final(device):
        return pltpu.make_async_remote_copy(
            stage.at[2], va.at[body], sw_s.at[3], sw_r.at[3], device_id=device, device_id_type=MESH)

    def far_copies(device):
        return [
            pltpu.make_async_remote_copy(
                stage.at[1], capx.at[body], id_s.at[0], id_r.at[0], device_id=device, device_id_type=MESH),
            pltpu.make_async_remote_copy(
                stage.at[0, pl.ds(8, 8)], condx.at[pl.ds(W + 9, 8)], id_s.at[1], id_r.at[1],
                device_id=device, device_id_type=MESH),
        ]

    below = device_of(group, row - 1 + SLABS * (row == 0))
    above = device_of(group, (row + 1) % SLABS)
    has_below = row > 0
    has_above = row < SLABS - 1

    def ghost_copies(side, with_start):
        if side == 0:
            device = below
            pairs = [(condx, pl.ds(W + 1, W + 1), pl.ds(W + 1 + X, W + 1))]
            cut, put = pl.ds(W, W), pl.ds(W + X, W)
        else:
            device = above
            pairs = [(condx, pl.ds(X, W + 1), pl.ds(0, W + 1))]
            cut, put = pl.ds(X, W), pl.ds(0, W)
        pairs += [(capx, cut, put), (misx, cut, put)]
        if with_start:
            pairs = [(va, cut, put)]
        return [
            pltpu.make_async_remote_copy(
                ref.at[a], ref.at[b], hs_s.at[side, n + 3 * with_start], hs_r.at[side, n + 3 * with_start],
                device_id=device, device_id_type=MESH)
            for n, (ref, a, b) in enumerate(pairs)
        ]

    def both_sides(act):
        @pl.when(has_below)
        def _():
            act(0)

        @pl.when(has_above)
        def _():
            act(1)

    def ghost_start():
        def act(side):
            for copy in ghost_copies(side, 0):
                copy.start()

            @pl.when(group == last)
            def _():
                ghost_copies(side, 1)[0].start()

        both_sides(act)

    @pl.when(swapped)
    def _():
        for copy in swap_copies(partner):
            copy.start()

        @pl.when((x_hi == 1) & (x_lo == 0))
        def _():
            swap_final(partner).start()

    @pl.when(jnp.logical_not(swapped))
    def _():
        for copy in far_copies(far):
            copy.start()

        def put(r, c):
            condx[W + 1 + r] = stage[0, r]
            capx[W + r] = stage[1, r]
            misx[W + r] = stage[3, r]
            return c

        lax.fori_loop(0, X, put, 0)
        planx[...] = plan_ref[...]

        @pl.when(group == last)
        def _():
            def put_final(r, c):
                va[W + r] = stage[2, r]
                return c

            lax.fori_loop(0, X, put_final, 0)

        ghost_start()

    def outside(lo_cond, lo):
        condx[pl.ds(lo_cond, W + 1)] = jnp.zeros((W + 1, Z, 8, 128), F32)
        capx[pl.ds(lo, W)] = jnp.ones((W, Z, 8, 128), F32)
        misx[pl.ds(lo, W)] = jnp.zeros((W, Z, 8, 128), F32)
        va[pl.ds(lo, W)] = jnp.zeros((W, Z, 8, 128), F32)

    @pl.when(jnp.logical_not(has_below))
    def _():
        outside(0, 0)

    @pl.when(jnp.logical_not(has_above))
    def _():
        outside(W + 1 + X, W + X)

    def gather_wait(k, c):
        gather_copy(k, (slab - k + SLABS) % SLABS).wait_recv()
        return c

    lax.fori_loop(1, SLABS, gather_wait, 0)
    nothing = jnp.zeros((8, 128), F32)
    for ref in (ck, ga, gb):
        ref[0] = nothing
        ref[SLABS + 1] = nothing

    def coarse_root(r, c):
        ck[r + 1] = jnp.sqrt(cbuf[r, 0])
        return c

    lax.fori_loop(0, SLABS, coarse_root, 0)
    CH = 8

    def chunk_rows(f):
        def step(n, c):
            f(n * CH)
            return c

        lax.fori_loop(0, SLABS // CH, step, 0)

    shape = (CH, 8, 128)

    def coarse_coefficients(r):
        k = ck[pl.ds(r + 1, CH)]
        column_of = iota(shape, 2) % CY
        layer = iota(shape, 1) + 8 * (iota(shape, 2) // CY)
        zero = jnp.zeros(shape, F32)
        scale = float(CF * CF)
        faces = [
            k * ck[pl.ds(r, CH)],
            k * ck[pl.ds(r + 2, CH)],
            jnp.where(column_of == 0, zero, k * pltpu.roll(k, 1, 2)),
            jnp.where(column_of == CY - 1, zero, k * pltpu.roll(k, 127, 2)),
            jnp.where(layer == 0, zero, scale * k * cz_below(k)),
            jnp.where(layer == Z - 1, zero, scale * k * cz_above(k)),
        ]
        store = cbuf[pl.ds(r, CH), 1] * float(CF * CF // STEPS)
        total = store
        for t in faces:
            total = total + t
        inverse = 1.0 / total
        for n in range(6):
            cco[n, pl.ds(r, CH)] = faces[n] * inverse
        cst[pl.ds(r, CH)] = store * inverse

    chunk_rows(coarse_coefficients)

    def coarse_sweep(src, dst):
        def rows(r):
            v = src[pl.ds(r + 1, CH)]
            c = pl.ds(r, CH)
            new = gbi[c] + cco[0, c] * src[pl.ds(r, CH)] + cco[1, c] * src[pl.ds(r + 2, CH)]
            new = new + (cco[2, c] * pltpu.roll(v, 1, 2) + cco[3, c] * pltpu.roll(v, 127, 2))
            new = new + (cco[4, c] * cz_below(v) + cco[5, c] * cz_above(v))
            dst[pl.ds(r + 1, CH)] = new

        chunk_rows(rows)

    def coarse_step():
        gbi[...] = cst[...] * ga[pl.ds(1, SLABS)]

        def pair(n, c):
            coarse_sweep(ga, gb)
            coarse_sweep(gb, ga)
            return c

        lax.fori_loop(0, SWEEPS // 2, pair, 0)

    ga[pl.ds(1, SLABS)] = cbuf[:, 2]

    def predict(n, c):
        coarse_step()
        return c

    lax.fori_loop(0, last - group, predict, 0)

    def extend(rows):
        flat = jnp.concatenate([part for c8 in rows for part in (c8[:, :CY], c8[:, CY:])], axis=0)
        for s in range(8):
            pick = (iota((CY, 128), 0) == 8 * s + iota((CY, 128), 1) // CF).astype(F32)
            wide = jnp.dot(flat, pick, preferred_element_type=F32, precision=EXACT)
            for n in range(len(rows)):
                pw[n, :, s, :] = wide[Z * n:Z * (n + 1)]

    @pl.when(group < last)
    def _():
        extend([ga[row], ga[row + 1], ga[row + 2]])
        for r in range(NR):
            va[r] = pw[0 if r < W else (1 if r < W + X else 2)]

    coarse_step()
    adv[...] = ga[row + 1]

    @pl.when(swapped)
    def _():
        for copy in swap_copies(partner) + far_copies(far):
            copy.wait_recv()

        @pl.when(group == last)
        def _():
            swap_final(partner).wait_recv()

        ghost_start()

    def ghost_wait(side):
        for copy in ghost_copies(1 - side, 0):
            copy.wait_recv()

        @pl.when(group == last)
        def _():
            ghost_copies(1 - side, 1)[0].wait_recv()

    both_sides(ghost_wait)

    def ghost_sent(side):
        for copy in ghost_copies(side, 0):
            copy.wait_send()

        @pl.when(group == last)
        def _():
            ghost_copies(side, 1)[0].wait_send()

    both_sides(ghost_sent)

    def root(r, c):
        condx[r] = jnp.sqrt(condx[r])
        return c

    lax.fori_loop(0, NR + 2, root, 0)
    fine = (Z, 8, 128)

    def coefficients(r, c):
        k = condx[r + 1]
        y = iota(fine, 1) * 128 + iota(fine, 2)
        zero = jnp.zeros(fine, F32)
        edge = jnp.zeros((1, 8, 128), F32)
        faces = [
            k * condx[r],
            k * condx[r + 2],
            jnp.where(y == 0, zero, k * y_below(k)),
            jnp.where(y == 1023, zero, k * y_above(k)),
            k * jnp.concatenate([edge, k[:-1]], 0),
            k * jnp.concatenate([k[1:], edge], 0),
        ]
        total = capx[r]
        for t in faces:
            total = total + t
        inverse = 1.0 / total
        inv[r] = inverse
        for n in range(6):
            co[n, r] = faces[n] * inverse
        return c

    lax.fori_loop(0, NR, coefficients, 0)

    def sweep(src, dst, lo, hi):
        def rows(r, c):
            v = src[r]
            new = (bi[r] + co[0, r] * src[r - 1]) + co[1, r] * src[r + 1]
            new = new + (co[4, r] * z_below(v) + co[5, r] * z_above(v))
            dst[r] = new + (co[2, r] * y_below(v) + co[3, r] * y_above(v))
            return c

        lax.fori_loop(lo, hi, rows, 0, unroll=2)

    def source(r, c):
        bi[r] = (capx[r] * va[r] + misx[r]) * inv[r]
        return c

    def sample(first):
        cell = wells_ref[...] - row * (X * Z * 1024)
        line = cell >> 7

        def part(n, c):
            v = va[pl.ds(W + 2 * n, 2)].reshape(256, 128)
            high = v.astype(BF16)
            rest = v - high.astype(F32)
            mid = rest.astype(BF16)
            low = (rest - mid.astype(F32)).astype(BF16)
            pieces = jnp.concatenate([high, mid, low], axis=1)
            hot = jnp.where(iota((256, 1024), 0) + 256 * n == line, 1.0, 0.0).astype(BF16)
            acc[...] += lax.dot_general(pieces, hot, (((0,), (0,)), ((), ())), preferred_element_type=F32)
            return c

        acc[...] = jnp.zeros(acc.shape, F32)
        lax.fori_loop(0, X // 2, part, 0)
        lines = acc[pl.ds(0, 128)] + acc[pl.ds(128, 128)] + acc[pl.ds(256, 128)]
        mine = jnp.where(iota((128, 1024), 0) == (cell & 127), lines, 0.0)
        got = jnp.sum(mine, axis=0, keepdims=True)
        sums[...] = got if first else sums[...] + got

    def exchange_copies(n, side):
        device, cut = (below, pl.ds(W, W)) if side == 0 else (above, pl.ds(X, W))
        return pltpu.make_async_remote_copy(
            va.at[cut], rx.at[n, 1 - side], ex_s.at[n, side], ex_r.at[n, 1 - side],
            device_id=device, device_id_type=MESH)

    per_step = SWEEPS // W
    for n in range(STEPS * per_step):
        if n % per_step == 0:
            lax.fori_loop(0, NR, source, 0)
        for k in range(1, W + 1):
            src, dst = (va, vb) if k % 2 else (vb, va)
            sweep(src, dst, k, NR - k)
        if n < NEX:
            both_sides(lambda side: exchange_copies(n, side).start())
        if n % per_step == per_step - 1:
            if n == STEPS * per_step - 1:
                @pl.when(swapped)
                def _():
                    own_copy = pltpu.make_async_remote_copy(
                        va.at[body], own, own_s, own_r, device_id=partner, device_id_type=MESH)
                    own_copy.start()
            sample(n // per_step == 0)
        if n < NEX:
            def arrive(side):
                exchange_copies(n, 1 - side).wait_recv()
                put = pl.ds(0, W) if side == 0 else pl.ds(W + X, W)
                va[put] = rx[n, side]
                exchange_copies(n, side).wait_send()

            both_sides(arrive)

    st1[group, 0] = restrict(va[body]) - adv[...]
    tot[...] = sums[...] * planx[...]
    for j in range(8):
        st1[group, 1, j:j + 1, :] = tot[:, 128 * j:128 * (j + 1)]

    def group_copy(k, who):
        return pltpu.make_async_remote_copy(
            st1.at[who], st1.at[who], e1_s.at[k], e1_r.at[k],
            device_id=device_of((group + k) % GROUPS, row), device_id_type=MESH)

    for k in range(1, GROUPS):
        group_copy(k, group).start()
    for k in range(1, GROUPS):
        group_copy(k, (group - k + GROUPS) % GROUPS).wait_recv()
    for g in range(1, GROUPS):
        st2[row, g - 1] = st1[g, 0]
    st2[row, 3] = (st1[0, 1] + st1[1, 1]) + (st1[2, 1] + st1[3, 1])

    def row_copy(k, who):
        return pltpu.make_async_remote_copy(
            st2.at[who], st2.at[who], e2_s.at[k], e2_r.at[k],
            device_id=device_of(group, (row + k) % SLABS), device_id_type=MESH)

    def row_start(k, c):
        row_copy(k, row).start()
        return c

    def row_wait(k, c):
        row_copy(k, (row - k + SLABS) % SLABS).wait_recv()
        return c

    lax.fori_loop(1, SLABS, row_start, 0)
    lax.fori_loop(1, SLABS, row_wait, 0)

    grad_ref[...] = jnp.sum(st2[:, 3], axis=0) * (1.0 / (STEPS * GROUPS))

    ga[pl.ds(1, SLABS)] = st2[:, 2]
    chain = last - period

    def correct(n, c):
        coarse_step()

        @pl.when(n < chain - 1)
        def _():
            ga[pl.ds(1, SLABS)] = ga[pl.ds(1, SLABS)] + st2[:, 1 - n]

        return c

    lax.fori_loop(0, chain, correct, 0)
    carried = jnp.where(chain > 0, 1.0, 0.0) * ga[slab + 1]
    extend([carried])

    @pl.when(swapped)
    def _():
        own_copy = pltpu.make_async_remote_copy(
            va.at[body], own, own_s, own_r, device_id=partner, device_id_type=MESH)
        own_copy.wait()

        def add(r, c):
            vb[W + r] = own[r] + pw[0]
            return c

        lax.fori_loop(0, X, add, 0)

    @pl.when(jnp.logical_not(swapped))
    def _():
        def add(r, c):
            vb[W + r] = va[W + r] + pw[0]
            return c

        lax.fori_loop(0, X, add, 0)

    outs = [
        pltpu.make_async_copy(vb.at[body, :, j, :], out_hbm.at[:, :, pl.ds(128 * j, 128)], out_sem.at[j])
        for j in range(8)
    ]
    for copy in outs:
        copy.start()

    def gather_sent(k, c):
        gather_copy(k, slab).wait_send()
        row_copy(k, row).wait_send()
        return c

    lax.fori_loop(1, SLABS, gather_sent, 0)
    for k in range(1, GROUPS):
        group_copy(k, group).wait_send()

    @pl.when(swapped)
    def _():
        for copy in swap_copies(partner):
            copy.wait_send()

        @pl.when((x_hi == 1) & (x_lo == 0))
        def _():
            swap_final(partner).wait_send()

    @pl.when(jnp.logical_not(swapped))
    def _():
        for copy in far_copies(far):
            copy.wait_send()

    for copy in outs:
        copy.wait()


def shards(final_level, misfit, conductivity, capacity, wells, plan):
    field = lambda *lead: pltpu.VMEM(lead + (Z, 8, 128), F32)
    tile = lambda *lead: pltpu.VMEM(lead + (8, 128), F32)
    dma = lambda *shape: pltpu.SemaphoreType.DMA(shape)
    vmem = pl.BlockSpec(memory_space=pltpu.VMEM)
    hbm = pl.BlockSpec(memory_space=pl.ANY)
    corrected, grad = pl.pallas_call(
        kernel,
        out_shape=(
            jax.ShapeDtypeStruct((X, Z, 1024), F32),
            jax.ShapeDtypeStruct((8, 128), F32),
        ),
        in_specs=[hbm, hbm, hbm, hbm, vmem, vmem],
        out_specs=(hbm, vmem),
        scratch_shapes=[
            field(4, X), field(NR + 2), field(NR), field(NR), field(NR), field(NR), field(6, NR), field(NR), field(NR),
            field(X), field(NEX, 2, W),
            tile(SLABS, 3), tile(SLABS + 2), tile(6, SLABS), tile(SLABS), tile(SLABS),
            tile(SLABS + 2), tile(SLABS + 2), tile(SLABS), field(), field(3), tile(),
            pltpu.VMEM((1, 1024), F32), pltpu.VMEM((384, 1024), F32), pltpu.VMEM((1, 1024), F32),
            pltpu.VMEM((1, 1024), F32), tile(GROUPS, 2), tile(SLABS, 4),
            dma(4, 8), dma(SLABS), dma(SLABS), dma(4), dma(4), dma(2), dma(2), dma(2, 4), dma(2, 4),
            dma(NEX, 2), dma(NEX, 2), dma(GROUPS), dma(GROUPS), dma(SLABS), dma(SLABS),
            pltpu.SemaphoreType.DMA, pltpu.SemaphoreType.DMA, dma(8),
        ],
        compiler_params=pltpu.CompilerParams(
            collective_id=0, has_side_effects=True, vmem_limit_bytes=60 * 2**20
        ),
    )(
        final_level, misfit[0], conductivity, capacity,
        wells.reshape(1, -1), plan.astype(F32),
    )
    return corrected[None], grad.reshape(-1)


def solution(mesh):
    return jax.shard_map(
        shards,
        mesh=mesh,
        in_specs=(
            P("slab", None, None),
            P("period", "slab", None, None),
            P("slab", None, None),
            P("slab", None, None),
            P(),
            P("period", None),
        ),
        out_specs=(P("period", "slab", None, None), P()),
        check_vma=False,
    )
```

```python
import jax
import jax.numpy as jnp
from jax import lax
from jax.experimental import pallas as pl
from jax.experimental.pallas import tpu as pltpu
from jax.sharding import PartitionSpec as P

MESH = pl.DeviceIdType.MESH
F32 = jnp.float32
BF16 = jnp.bfloat16
STEPS = 2
SWEEPS = 8
CF = 16
X = 16
Z = 16
SLABS = 32
GROUPS = 4
W = 4
NR = X + 2 * W
NEX = STEPS * SWEEPS // W - 1
CY = 64
EXACT = lax.Precision.HIGHEST


def iota(shape, dim):
    return lax.broadcasted_iota(jnp.int32, shape, dim)


def y_below(v):
    rolled = pltpu.roll(v, 1, 2)
    return jnp.where(iota(v.shape, 2) == 0, pltpu.roll(rolled, 1, 1), rolled)


def y_above(v):
    rolled = pltpu.roll(v, 127, 2)
    return jnp.where(iota(v.shape, 2) == 127, pltpu.roll(rolled, 7, 1), rolled)


LAYERS = [z for h in range(2) for z in range(h, Z, 2)]


def cz_both(v):
    turned = pltpu.roll(v, 64, 2)
    upper = iota(v.shape, 2) >= 64
    below = jnp.where(upper, turned, pltpu.roll(turned, 1, 1))
    above = jnp.where(upper, pltpu.roll(turned, 7, 1), turned)
    return below, above


def device_of(group, row):
    return (2 * (group // 2) + row % 2, 2 * (row // 2) + group % 2)


def kernel(
    final_hbm, misfit_hbm, cond_hbm, cap_hbm, wells_ref, plan_ref,
    out_hbm, grad_ref,
    stage, condx, capx, misx, va, vb, co, inv, bi, own, tx, rx,
    cbuf, crow, ck, cco, cst, ga, gb, gbi, rs, pw, fore, adv, planx, acc, sums, tot, st1, st2, st3,
    ld_sem, cr_s, cr_r, ag_s, ag_r, sw_s, sw_r, hs_s, hs_r, ex_s, ex_r, e1_s, e1_r, e2_s, e2_r, e3_s, e3_r,
    own_s, own_r, out_sem,
):
    period = lax.axis_index("period")
    slab = lax.axis_index("slab")
    x_hi, core = period // 2, period % 2
    column, x_lo = slab // 2, slab % 2
    group = 2 * x_hi + x_lo
    row = 2 * column + core
    swapped = core != x_lo
    partner = (2 * x_hi + 1 - core, 2 * column + 1 - x_lo)
    far = (2 * (1 - x_hi) + core, 2 * column + 1 - x_lo)
    last = GROUPS - 1

    def load(k):
        src = (cond_hbm, cap_hbm, final_hbm, misfit_hbm)[k]
        return [
            pltpu.make_async_copy(src.at[:, :, pl.ds(128 * j, 128)], stage.at[k, :, :, j, :], ld_sem.at[k, j])
            for j in range(8)
        ]

    loads = [load(k) for k in range(4)]
    for group_of in loads:
        for copy in group_of:
            copy.start()

    barrier = pltpu.get_barrier_semaphore()

    def hello(device):
        pl.semaphore_signal(barrier, inc=1, device_id=device, device_id_type=MESH)

    def greet(k, c):
        hello(device_of(group, (row + k) % SLABS))
        return c

    lax.fori_loop(1, SLABS, greet, 0)
    for k in range(1, GROUPS):
        hello(device_of((group + k) % GROUPS, row))

    @pl.when(swapped)
    def _():
        hello(partner)

    fine_lane = iota((128, CY), 0)
    coarse_lane = iota((128, CY), 1)

    def restrict(block):
        summed = jnp.sum(block, axis=0)
        rs[...] = jnp.concatenate([summed[z:z + 1] for z in LAYERS], axis=0)
        total = jnp.zeros((Z, CY), F32)
        for s in range(8):
            pick = (coarse_lane == 8 * s + fine_lane // CF).astype(F32)
            total = total + jnp.dot(rs[:, s, :], pick, preferred_element_type=F32, precision=EXACT)
        total = total * (1.0 / (CF * CF))
        return jnp.concatenate([total[:8], total[8:]], axis=1)

    for k in (0, 1, 2):
        for copy in loads[k]:
            copy.wait()
        crow[k] = restrict(stage[k])

    pl.semaphore_wait(barrier, (SLABS - 1) + GROUPS - 1 + swapped.astype(jnp.int32))

    def trade_rows():
        return pltpu.make_async_remote_copy(
            crow, cbuf.at[2 * column + x_lo], cr_s, cr_r, device_id=partner, device_id_type=MESH)

    def gather_copy(k, who):
        return pltpu.make_async_remote_copy(
            cbuf.at[who], cbuf.at[who], ag_s.at[k], ag_r.at[k],
            device_id=device_of(group, (row + k) % SLABS), device_id_type=MESH)

    def gather_start():
        def start(k, c):
            gather_copy(k, row).start()
            return c

        lax.fori_loop(1, SLABS, start, 0)

    body = pl.ds(W, X)

    def trade(k, ref, shift, n, lo, rows, device):
        return pltpu.make_async_remote_copy(
            stage.at[k, pl.ds(lo, rows)], ref.at[pl.ds(shift + lo, rows)], sw_s.at[n], sw_r.at[n],
            device_id=device, device_id_type=MESH)

    def trade_mis(d):
        return [trade(3, misx, W, 0, 0, W, d), trade(3, misx, W, 1, X - W, W, d)], [trade(3, misx, W, 2, W, X - 2 * W, d)]

    def trade_cap(d):
        return [trade(1, capx, W, 3, 0, W, d), trade(1, capx, W, 4, X - W, W, d)], [trade(1, capx, W, 5, W, X - 2 * W, d)]

    def trade_low(d):
        return [trade(0, condx, W + 1, 6, 0, W + 1, d)], [trade(0, condx, W + 1, 7, W + 1, X // 2 - W - 1, d)]

    def trade_high(d):
        return [trade(0, condx, W + 1, 8, X - W - 1, W + 1, d)], [trade(0, condx, W + 1, 9, X // 2, X // 2 - W - 1, d)]

    def trade_end(d):
        return [trade(2, va, W, 10, 0, W, d), trade(2, va, W, 11, X - W, W, d)], [trade(2, va, W, 12, W, X - 2 * W, d)]

    plan_copy = pltpu.make_async_remote_copy(
        plan_ref, planx, sw_s.at[13], sw_r.at[13], device_id=partner, device_id_type=MESH)
    to_last = (x_hi == 1) & (x_lo == 0)
    far_last = (x_hi == 0) & (x_lo == 0)

    def each(act, *lists):
        for part in range(2):
            for pair in lists:
                for copy in pair[part]:
                    act(copy)

    def outgoing(act):
        @pl.when(swapped & to_last)
        def _():
            each(act, trade_mis(partner), trade_end(partner))

        @pl.when(swapped & jnp.logical_not(to_last))
        def _():
            each(act, trade_mis(partner), trade_low(partner))

        @pl.when(swapped)
        def _():
            act(plan_copy)

        @pl.when(jnp.logical_not(swapped) & far_last)
        def _():
            each(act, trade_cap(far), trade_low(far), trade_high(far))

        @pl.when(jnp.logical_not(swapped) & jnp.logical_not(far_last))
        def _():
            each(act, trade_cap(far), trade_high(far))

    def incoming(part):
        for pair in (trade_cap(far), trade_high(far), trade_low(far), trade_mis(partner)):
            for copy in pair[part]:
                copy.wait_recv()

        @pl.when(group == last)
        def _():
            for copy in trade_end(partner)[part]:
                copy.wait_recv()

    below = device_of(group, (row + SLABS - 1) % SLABS)
    above = device_of(group, (row + 1) % SLABS)
    has_below = row > 0
    has_above = row < SLABS - 1

    def ghost_copies(side, with_start):
        if side == 0:
            device = below
            pairs = [(condx, pl.ds(W + 1, W + 1), pl.ds(W + 1 + X, W + 1))]
            cut, put = pl.ds(W, W), pl.ds(W + X, W)
        else:
            device = above
            pairs = [(condx, pl.ds(X, W + 1), pl.ds(0, W + 1))]
            cut, put = pl.ds(X, W), pl.ds(0, W)
        pairs += [(capx, cut, put), (misx, cut, put)]
        if with_start:
            pairs = [(va, cut, put)]
        return [
            pltpu.make_async_remote_copy(
                tx.at[side] if with_start else ref.at[a], ref.at[b],
                hs_s.at[side, n + 3 * with_start], hs_r.at[side, n + 3 * with_start],
                device_id=device, device_id_type=MESH)
            for n, (ref, a, b) in enumerate(pairs)
        ]

    def both_sides(act):
        @pl.when(has_below)
        def _():
            act(0)

        @pl.when(has_above)
        def _():
            act(1)

    def ghost_start():
        def act(side):
            for copy in ghost_copies(side, 0):
                copy.start()

            @pl.when(group == last)
            def _():
                tx[side] = va[pl.ds(W, W) if side == 0 else pl.ds(X, W)]
                ghost_copies(side, 1)[0].start()

        both_sides(act)

    def ghost_wait():
        def arrived(side):
            for copy in ghost_copies(1 - side, 0):
                copy.wait_recv()

            @pl.when(group == last)
            def _():
                ghost_copies(1 - side, 1)[0].wait_recv()

        both_sides(arrived)

    def ghost_sent():
        def act(side):
            for copy in ghost_copies(side, 0):
                copy.wait_send()

            @pl.when(group == last)
            def _():
                ghost_copies(side, 1)[0].wait_send()

        both_sides(act)

    fine = (Z, 8, 128)

    def coefficients(lo, hi):
        def one(r, c):
            k = jnp.sqrt(condx[r + 1])
            y = iota(fine, 1) * 128 + iota(fine, 2)
            zero = jnp.zeros(fine, F32)
            edge = jnp.zeros((1, 8, 128), F32)
            faces = [
                k * jnp.sqrt(condx[r]),
                k * jnp.sqrt(condx[r + 2]),
                jnp.where(y == 0, zero, k * y_below(k)),
                jnp.where(y == 1023, zero, k * y_above(k)),
                k * jnp.concatenate([edge, k[:-1]], 0),
                k * jnp.concatenate([k[1:], edge], 0),
            ]
            total = capx[r]
            for t in faces:
                total = total + t
            inverse = 1.0 / total
            inv[r] = inverse
            for n in range(6):
                co[n, r] = faces[n] * inverse
            return c

        lax.fori_loop(lo, hi, one, 0)

    for copy in loads[3]:
        copy.wait()

    @pl.when(swapped)
    def _():
        trade_rows().start()

    @pl.when(jnp.logical_not(swapped))
    def _():
        cbuf[row] = crow[...]
        gather_start()

    outgoing(lambda copy: copy.start())

    @pl.when(swapped)
    def _():
        pltpu.make_async_remote_copy(
            crow, cbuf.at[row], cr_s, cr_r, device_id=partner, device_id_type=MESH).wait_recv()
        gather_start()

    def outside(lo_cond, lo):
        condx[pl.ds(lo_cond, W + 1)] = jnp.zeros((W + 1, Z, 8, 128), F32)
        capx[pl.ds(lo, W)] = jnp.ones((W, Z, 8, 128), F32)
        misx[pl.ds(lo, W)] = jnp.zeros((W, Z, 8, 128), F32)
        va[pl.ds(lo, W)] = jnp.zeros((W, Z, 8, 128), F32)

    @pl.when(jnp.logical_not(has_below))
    def _():
        outside(0, 0)

    @pl.when(jnp.logical_not(has_above))
    def _():
        outside(W + 1 + X, W + X)

    @pl.when(jnp.logical_not(swapped))
    def _():
        def put(r, c):
            condx[W + 1 + r] = stage[0, r]
            capx[W + r] = stage[1, r]
            misx[W + r] = stage[3, r]
            return c

        lax.fori_loop(0, X, put, 0)
        planx[...] = plan_ref[...]

        @pl.when(group == last)
        def _():
            def put_final(r, c):
                va[W + r] = stage[2, r]
                return c

            lax.fori_loop(0, X, put_final, 0)

        ghost_start()

    def gather_wait(k, c):
        gather_copy(k, (row - k + SLABS) % SLABS).wait_recv()
        return c

    lax.fori_loop(1, SLABS, gather_wait, 0)
    nothing = jnp.zeros((8, 128), F32)
    for ref in (ck, ga, gb):
        ref[0] = nothing
        ref[SLABS + 1] = nothing

    def coarse_root(r, c):
        ck[r + 1] = jnp.sqrt(cbuf[r, 0])
        return c

    lax.fori_loop(0, SLABS, coarse_root, 0)
    CH = 8
    shape = (CH, 8, 128)

    def coarse_coefficients(r):
        k = ck[pl.ds(r + 1, CH)]
        column_of = iota(shape, 2) % CY
        layer = 2 * iota(shape, 1) + iota(shape, 2) // CY
        zero = jnp.zeros(shape, F32)
        scale = float(CF * CF)
        k_below, k_above = cz_both(k)
        faces = [
            k * ck[pl.ds(r, CH)],
            k * ck[pl.ds(r + 2, CH)],
            jnp.where(column_of == 0, zero, k * pltpu.roll(k, 1, 2)),
            jnp.where(column_of == CY - 1, zero, k * pltpu.roll(k, 127, 2)),
            jnp.where(layer == 0, zero, scale * k * k_below),
            jnp.where(layer == Z - 1, zero, scale * k * k_above),
        ]
        store = cbuf[pl.ds(r, CH), 1] * float(CF * CF // STEPS)
        total = store
        for t in faces:
            total = total + t
        inverse = 1.0 / total
        for n in range(6):
            cco[n, pl.ds(r, CH)] = faces[n] * inverse
        cst[pl.ds(r, CH)] = store * inverse

    for n in range(SLABS // CH):
        coarse_coefficients(n * CH)

    def coarse_sweep(src, dst):
        for n in range(SLABS // CH):
            r = n * CH
            v = src[pl.ds(r + 1, CH)]
            c = pl.ds(r, CH)
            v_below, v_above = cz_both(v)
            new = gbi[c] + cco[0, c] * src[pl.ds(r, CH)] + cco[1, c] * src[pl.ds(r + 2, CH)]
            new = new + (cco[2, c] * pltpu.roll(v, 1, 2) + cco[3, c] * pltpu.roll(v, 127, 2))
            dst[pl.ds(r + 1, CH)] = new + (cco[4, c] * v_below + cco[5, c] * v_above)

    def coarse_step():
        gbi[...] = cst[...] * ga[pl.ds(1, SLABS)]

        def pair(n, c):
            coarse_sweep(ga, gb)
            coarse_sweep(gb, ga)
            return c

        lax.fori_loop(0, SWEEPS // 2, pair, 0)

    @pl.when(swapped)
    def _():
        incoming(0)
        ghost_start()

    ga[pl.ds(1, SLABS)] = cbuf[:, 2]

    def predict(n, c):
        for k in range(3):
            fore[k] = ga[row + k]
        coarse_step()
        return c

    lax.fori_loop(0, last - group + 1, predict, 0)
    adv[...] = ga[row + 1]

    def extend(rows):
        flat = jnp.concatenate([part for c8 in rows for part in (c8[:, :CY], c8[:, CY:])], axis=0)
        for s in range(8):
            pick = (iota((CY, 128), 0) == 8 * s + iota((CY, 128), 1) // CF).astype(F32)
            wide = jnp.dot(flat, pick, preferred_element_type=F32, precision=EXACT)
            for n in range(len(rows)):
                pw[n, :, s, :] = wide[Z * n:Z * (n + 1)]

    def repeated(n):
        block = pw[n]
        places = [LAYERS.index(z) for z in range(Z)]
        return jnp.concatenate([block[p:p + 1] for p in places], axis=0)

    @pl.when(group < last)
    def _():
        extend([fore[0], fore[1], fore[2]])
        for part, (lo, hi) in enumerate(((0, W), (W, W + X), (W + X, NR))):
            rows = repeated(part)
            for r in range(lo, hi):
                va[r] = rows

    @pl.when(swapped)
    def _():
        incoming(1)
        plan_copy.wait_recv()

    coefficients(W + 1, W + X - 1)

    def sweep(src, dst, rows):
        for r in rows:
            for z in range(0, Z, 2):
                here = pl.ds(z, 2)
                v = src[r, here]
                if z == 0:
                    z_below = jnp.concatenate([v[:1], v[:1]], 0)
                else:
                    z_below = src[r, pl.ds(z - 1, 2)]
                if z == Z - 2:
                    z_above = jnp.concatenate([v[1:], v[1:]], 0)
                else:
                    z_above = src[r, pl.ds(z + 1, 2)]
                new = (bi[r, here] + co[0, r, here] * src[r - 1, here]) + co[1, r, here] * src[r + 1, here]
                new = new + (co[4, r, here] * z_below + co[5, r, here] * z_above)
                dst[r, here] = new + (co[2, r, here] * y_below(v) + co[3, r, here] * y_above(v))

    def source(lo, hi):
        def one(r, c):
            bi[r] = (capx[r] * va[r] + misx[r]) * inv[r]
            return c

        lax.fori_loop(lo, hi, one, 0)

    def sample():
        cell = wells_ref[...] - row * (X * Z * 1024)
        line = cell >> 7

        def part(n, c):
            v = va[pl.ds(W + 2 * n, 2)].reshape(256, 128)
            high = v.astype(BF16)
            rest = v - high.astype(F32)
            mid = rest.astype(BF16)
            low = (rest - mid.astype(F32)).astype(BF16)
            pieces = jnp.concatenate([high, mid, low], axis=1)
            hot = jnp.where(iota((256, 1024), 0) + 256 * n == line, 1.0, 0.0).astype(BF16)
            acc[...] += lax.dot_general(pieces, hot, (((0,), (0,)), ((), ())), preferred_element_type=F32)
            return c

        acc[...] = jnp.zeros(acc.shape, F32)
        lax.fori_loop(0, X // 2, part, 0)
        lines = acc[pl.ds(0, 128)] + acc[pl.ds(128, 128)] + acc[pl.ds(256, 128)]
        mine = jnp.where(iota((128, 1024), 0) == (cell & 127), lines, 0.0)
        sums[...] += jnp.sum(mine, axis=0, keepdims=True)

    def exchange_copy(n, side):
        return pltpu.make_async_remote_copy(
            tx.at[side], rx.at[n, 1 - side], ex_s.at[n, side], ex_r.at[n, 1 - side],
            device_id=below if side == 0 else above, device_id_type=MESH)

    sums[...] = jnp.zeros(sums.shape, F32)
    per_step = SWEEPS // W
    blocks = STEPS * per_step

    def block(n, c):
        opens = n % per_step == 0

        @pl.when(opens)
        def _():
            source(W + 1, W + X - 1)

        for k in range(1, W + 1):
            src, dst = (va, vb) if k % 2 else (vb, va)
            sweep(src, dst, range(W + k, W + X - k))

        @pl.when(n == 0)
        def _():
            ghost_wait()
            ghost_sent()
            coefficients(0, W + 1)
            coefficients(W + X - 1, NR)

        @pl.when(n > 0)
        def _():
            def arrive(side):
                exchange_copy(n - 1, 1 - side).wait_recv()
                va[pl.ds(0, W) if side == 0 else pl.ds(W + X, W)] = rx[n - 1, side]
                exchange_copy(n - 1, side).wait_send()

            both_sides(arrive)

        @pl.when(opens)
        def _():
            source(0, W + 1)
            source(W + X - 1, NR)

        for k in range(1, W + 1):
            src, dst = (va, vb) if k % 2 else (vb, va)
            sweep(src, dst, [*range(k, W + k), *range(W + X - k, NR - k)])

        @pl.when(n < blocks - 1)
        def _():
            tx[0] = va[pl.ds(W, W)]
            tx[1] = va[pl.ds(X, W)]
            both_sides(lambda side: exchange_copy(n, side).start())

        @pl.when((n % per_step == per_step - 1) & (n < blocks - 1))
        def _():
            sample()

        return c

    lax.fori_loop(0, blocks, block, 0)

    st1[group] = restrict(va[body]) - adv[...]

    def group_copy(ref, send, receive, k, who):
        return pltpu.make_async_remote_copy(
            ref.at[who], ref.at[who], send.at[k], receive.at[k],
            device_id=device_of((group + k) % GROUPS, row), device_id_type=MESH)

    def group_start(*how):
        for k in range(1, GROUPS):
            group_copy(*how, k, group).start()

    def group_wait(*how):
        for k in range(1, GROUPS):
            group_copy(*how, k, (group - k + GROUPS) % GROUPS).wait_recv()

    group_start(st1, e1_s, e1_r)
    own_copy = pltpu.make_async_remote_copy(
        va.at[body], own, own_s, own_r, device_id=partner, device_id_type=MESH)
    @pl.when(swapped)
    def _():
        own_copy.start()

    sample()
    tot[...] = sums[...] * planx[...]
    for j in range(8):
        st2[row, 3, j:j + 1, :] = tot[:, 128 * j:128 * (j + 1)]
    group_wait(st1, e1_s, e1_r)
    for g in range(1, GROUPS):
        st2[row, g - 1] = st1[g]

    def row_copy(k, who):
        return pltpu.make_async_remote_copy(
            st2.at[who], st2.at[who], e2_s.at[k], e2_r.at[k],
            device_id=device_of(group, (row + k) % SLABS), device_id_type=MESH)

    def row_start(k, c):
        row_copy(k, row).start()
        return c

    def row_wait(k, c):
        row_copy(k, (row - k + SLABS) % SLABS).wait_recv()
        return c

    lax.fori_loop(1, SLABS, row_start, 0)
    lax.fori_loop(1, SLABS, row_wait, 0)
    st3[group] = jnp.sum(st2[:, 3], axis=0)
    group_start(st3, e3_s, e3_r)

    ga[pl.ds(1, SLABS)] = st2[:, 2]
    chain = last - period

    def correct(n, c):
        coarse_step()

        @pl.when(n < chain - 1)
        def _():
            ga[pl.ds(1, SLABS)] = ga[pl.ds(1, SLABS)] + st2[:, 1 - n]

        return c

    lax.fori_loop(0, chain, correct, 0)
    carried = jnp.where(chain > 0, 1.0, 0.0) * ga[slab + 1]
    extend([carried])
    wide = repeated(0)

    @pl.when(swapped)
    def _():
        own_copy.wait()
        for r in range(X):
            vb[W + r] = own[r] + wide

    @pl.when(jnp.logical_not(swapped))
    def _():
        for r in range(X):
            vb[W + r] = va[W + r] + wide

    outs = [
        pltpu.make_async_copy(vb.at[body, :, j, :], out_hbm.at[:, :, pl.ds(128 * j, 128)], out_sem.at[j])
        for j in range(8)
    ]
    for copy in outs:
        copy.start()
    group_wait(st3, e3_s, e3_r)
    grad_ref[...] = ((st3[0] + st3[1]) + (st3[2] + st3[3])) * (1.0 / (STEPS * GROUPS))

    def rows_sent(k, c):
        gather_copy(k, row).wait_send()
        row_copy(k, row).wait_send()
        return c

    lax.fori_loop(1, SLABS, rows_sent, 0)
    for k in range(1, GROUPS):
        group_copy(st1, e1_s, e1_r, k, group).wait_send()
        group_copy(st3, e3_s, e3_r, k, group).wait_send()
    outgoing(lambda copy: copy.wait_send())

    @pl.when(swapped)
    def _():
        trade_rows().wait_send()

    for copy in outs:
        copy.wait()


def shards(final_level, misfit, conductivity, capacity, wells, plan):
    field = lambda *lead: pltpu.VMEM(lead + (Z, 8, 128), F32)
    tile = lambda *lead: pltpu.VMEM(lead + (8, 128), F32)
    dma = lambda *shape: pltpu.SemaphoreType.DMA(shape)
    vmem = pl.BlockSpec(memory_space=pltpu.VMEM)
    hbm = pl.BlockSpec(memory_space=pl.ANY)
    corrected, grad = pl.pallas_call(
        kernel,
        out_shape=(
            jax.ShapeDtypeStruct((X, Z, 1024), F32),
            jax.ShapeDtypeStruct((8, 128), F32),
        ),
        in_specs=[hbm, hbm, hbm, hbm, vmem, vmem],
        out_specs=(hbm, vmem),
        scratch_shapes=[
            field(4, X), field(NR + 2), field(NR), field(NR), field(NR), field(NR), field(6, NR), field(NR), field(NR),
            field(X), field(2, W), field(NEX, 2, W),
            tile(SLABS, 3), tile(3), tile(SLABS + 2), tile(6, SLABS), tile(SLABS),
            tile(SLABS + 2), tile(SLABS + 2), tile(SLABS), field(), field(3), tile(3), tile(),
            pltpu.VMEM((1, 1024), F32), pltpu.VMEM((384, 1024), F32), pltpu.VMEM((1, 1024), F32),
            pltpu.VMEM((1, 1024), F32), tile(GROUPS), tile(SLABS, 4), tile(GROUPS),
            dma(4, 8), pltpu.SemaphoreType.DMA, pltpu.SemaphoreType.DMA, dma(SLABS), dma(SLABS),
            dma(14), dma(14), dma(2, 4), dma(2, 4), dma(NEX, 2), dma(NEX, 2),
            dma(GROUPS), dma(GROUPS), dma(SLABS), dma(SLABS), dma(GROUPS), dma(GROUPS),
            pltpu.SemaphoreType.DMA, pltpu.SemaphoreType.DMA, dma(8),
        ],
        compiler_params=pltpu.CompilerParams(
            collective_id=0, has_side_effects=True, vmem_limit_bytes=60 * 2**20
        ),
    )(
        final_level, misfit[0], conductivity, capacity,
        wells.reshape(1, -1), plan.astype(F32),
    )
    return corrected[None], grad.reshape(-1)


def solution(mesh):
    return jax.shard_map(
        shards,
        mesh=mesh,
        in_specs=(
            P("slab", None, None),
            P("period", "slab", None, None),
            P("slab", None, None),
            P("slab", None, None),
            P(),
            P("period", None),
        ),
        out_specs=(P("period", "slab", None, None), P()),
        check_vma=False,
    )
```

```python
import jax
import jax.numpy as jnp
from jax import lax
from jax.experimental import pallas as pl
from jax.experimental.pallas import tpu as pltpu
from jax.sharding import PartitionSpec as P

MESH = pl.DeviceIdType.MESH
F32 = jnp.float32
BF16 = jnp.bfloat16
STEPS = 2
SWEEPS = 8
CF = 16
X = 16
Z = 16
SLABS = 32
GROUPS = 4
W = 4
NR = X + 2 * W
NEX = STEPS * SWEEPS // W - 1
CY = 64
EXACT = lax.Precision.HIGHEST


def iota(shape, dim):
    return lax.broadcasted_iota(jnp.int32, shape, dim)


def y_below(v):
    rolled = pltpu.roll(v, 1, 2)
    return jnp.where(iota(v.shape, 2) == 0, pltpu.roll(rolled, 1, 1), rolled)


def y_above(v):
    rolled = pltpu.roll(v, 127, 2)
    return jnp.where(iota(v.shape, 2) == 127, pltpu.roll(rolled, 7, 1), rolled)


LAYERS = [z for h in range(2) for z in range(h, Z, 2)]


def cz_both(v):
    turned = pltpu.roll(v, 64, 2)
    upper = iota(v.shape, 2) >= 64
    below = jnp.where(upper, turned, pltpu.roll(turned, 1, 1))
    above = jnp.where(upper, pltpu.roll(turned, 7, 1), turned)
    return below, above


def device_of(group, row):
    return (2 * (group // 2) + row % 2, 2 * (row // 2) + group % 2)


def kernel(
    final_hbm, misfit_hbm, cond_hbm, cap_hbm, wells_ref, plan_ref,
    out_hbm, grad_ref,
    stage, condx, capx, misx, va, vb, co, inv, bi, own, tx, rx,
    cbuf, crow, ck, cco, cst, ga, gb, gbi, rs, pw, fore, adv, plan_row, planx, rootx, acc, sums, tot, st1, st2, st3,
    ld_sem, cr_s, cr_r, ag_s, ag_r, sw_s, sw_r, hs_s, hs_r, ex_s, ex_r, e1_s, e1_r, e2_s, e2_r, e3_s, e3_r,
    own_s, own_r, out_sem,
):
    period = lax.axis_index("period")
    slab = lax.axis_index("slab")
    x_hi, core = period // 2, period % 2
    column, x_lo = slab // 2, slab % 2
    group = 2 * x_hi + x_lo
    row = 2 * column + core
    swapped = core != x_lo
    partner = (2 * x_hi + 1 - core, 2 * column + 1 - x_lo)
    far = (2 * (1 - x_hi) + core, 2 * column + 1 - x_lo)
    last = GROUPS - 1

    def load(k):
        src = (cond_hbm, cap_hbm, final_hbm, misfit_hbm)[k]
        return [
            pltpu.make_async_copy(src.at[:, :, pl.ds(128 * j, 128)], stage.at[k, :, :, j, :], ld_sem.at[k, j])
            for j in range(8)
        ]

    loads = [load(k) for k in range(4)]
    for group_of in loads:
        for copy in group_of:
            copy.start()

    barrier = pltpu.get_barrier_semaphore()

    def hello(device):
        pl.semaphore_signal(barrier, inc=1, device_id=device, device_id_type=MESH)

    def greet(k, c):
        hello(device_of(group, (row + k) % SLABS))
        return c

    lax.fori_loop(1, SLABS, greet, 0)
    for k in range(1, GROUPS):
        hello(device_of((group + k) % GROUPS, row))

    @pl.when(swapped)
    def _():
        hello(partner)

    def restrict(*blocks):
        for n, block in enumerate(blocks):
            summed = jnp.sum(block, axis=0)
            rs[pl.ds(Z * n, Z)] = jnp.concatenate([summed[z:z + 1] for z in LAYERS], axis=0)
        rows = Z * len(blocks)
        flat = jnp.concatenate([rs[pl.ds(0, rows), s, :] for s in range(8)], axis=1)
        pick = (iota((1024, CY), 1) == iota((1024, CY), 0) // CF).astype(F32)
        total = jnp.dot(flat, pick, preferred_element_type=F32, precision=EXACT) * (1.0 / (CF * CF))
        return [
            jnp.concatenate([total[Z * n:Z * n + 8], total[Z * n + 8:Z * n + Z]], axis=1)
            for n in range(len(blocks))
        ]

    for k in (0, 1):
        for copy in loads[k]:
            copy.wait()
    pl.semaphore_wait(barrier, (SLABS - 1) + GROUPS - 1 + swapped.astype(jnp.int32))

    def trade_rows():
        return pltpu.make_async_remote_copy(
            crow, cbuf.at[2 * column + x_lo], cr_s, cr_r, device_id=partner, device_id_type=MESH)

    def gather_copy(k, who):
        return pltpu.make_async_remote_copy(
            cbuf.at[who], cbuf.at[who], ag_s.at[k], ag_r.at[k],
            device_id=device_of(group, (row + k) % SLABS), device_id_type=MESH)

    def gather_start():
        def start(k, c):
            gather_copy(k, row).start()
            return c

        lax.fori_loop(1, SLABS, start, 0)

    body = pl.ds(W, X)

    def trade(k, ref, shift, n, lo, rows, device):
        return pltpu.make_async_remote_copy(
            stage.at[k, pl.ds(lo, rows)], ref.at[pl.ds(shift + lo, rows)], sw_s.at[n], sw_r.at[n],
            device_id=device, device_id_type=MESH)

    def trade_mis(d):
        return [trade(3, misx, W, 0, 0, W, d), trade(3, misx, W, 1, X - W, W, d)], [trade(3, misx, W, 2, W, X - 2 * W, d)]

    def trade_cap(d):
        return [trade(1, capx, W, 3, 0, W, d), trade(1, capx, W, 4, X - W, W, d)], [trade(1, capx, W, 5, W, X - 2 * W, d)]

    def trade_low(d):
        return [trade(0, condx, W + 1, 6, 0, W + 1, d)], [trade(0, condx, W + 1, 7, W + 1, X // 2 - W - 1, d)]

    def trade_high(d):
        return [trade(0, condx, W + 1, 8, X - W - 1, W + 1, d)], [trade(0, condx, W + 1, 9, X // 2, X // 2 - W - 1, d)]

    def trade_end(d):
        return [trade(2, va, W, 10, 0, W, d), trade(2, va, W, 11, X - W, W, d)], [trade(2, va, W, 12, W, X - 2 * W, d)]

    plan_copy = pltpu.make_async_remote_copy(
        plan_row, planx, sw_s.at[13], sw_r.at[13], device_id=partner, device_id_type=MESH)
    to_last = (x_hi == 1) & (x_lo == 0)
    far_last = (x_hi == 0) & (x_lo == 0)

    def in_order(*lists):
        return [copy for pairs in lists for part in range(2) for pair in pairs for copy in pair[part]]

    HEAD = 2

    def outgoing(act, lo=0, hi=None):
        @pl.when(swapped & to_last)
        def _():
            for copy in in_order([trade_cap(partner)], [trade_mis(partner)])[lo:hi]:
                act(copy)

        @pl.when(swapped & jnp.logical_not(to_last))
        def _():
            for copy in in_order([trade_low(partner)], [trade_mis(partner)])[lo:hi]:
                act(copy)

        @pl.when(jnp.logical_not(swapped) & far_last)
        def _():
            for copy in in_order([trade_low(far), trade_high(far)], [trade_end(far)])[lo:hi]:
                act(copy)

        @pl.when(jnp.logical_not(swapped) & jnp.logical_not(far_last))
        def _():
            for copy in in_order([trade_cap(far), trade_high(far)])[lo:hi]:
                act(copy)

    def incoming_data(part):
        for pair in (trade_cap(far), trade_high(far), trade_low(far)):
            for copy in pair[part]:
                copy.wait_recv()

    def incoming_source(part):
        for copy in trade_mis(partner)[part]:
            copy.wait_recv()

        @pl.when(group == last)
        def _():
            for copy in trade_end(partner)[part]:
                copy.wait_recv()

    below = device_of(group, (row + SLABS - 1) % SLABS)
    above = device_of(group, (row + 1) % SLABS)
    has_below = row > 0
    has_above = row < SLABS - 1

    def ghost_copies(side, names):
        device = below if side == 0 else above
        cut, put = (pl.ds(W, W), pl.ds(W + X, W)) if side == 0 else (pl.ds(X, W), pl.ds(0, W))
        wide_cut, wide_put = (
            (pl.ds(W + 1, W + 1), pl.ds(W + 1 + X, W + 1)) if side == 0 else (pl.ds(X, W + 1), pl.ds(0, W + 1)))
        table = {
            "cond": (0, condx.at[wide_cut], condx.at[wide_put]),
            "cap": (1, capx.at[cut], capx.at[put]),
            "mis": (2, misx.at[cut], misx.at[put]),
            "end": (3, tx.at[side], va.at[put]),
        }
        return [
            pltpu.make_async_remote_copy(
                table[name][1], table[name][2], hs_s.at[side, table[name][0]], hs_r.at[side, table[name][0]],
                device_id=device, device_id_type=MESH)
            for name in names
        ]

    def both_sides(act):
        @pl.when(has_below)
        def _():
            act(0)

        @pl.when(has_above)
        def _():
            act(1)

    DATA = ("cond", "cap")

    def ghost_data():
        def act(side):
            for copy in ghost_copies(side, DATA):
                copy.start()

        both_sides(act)

    def ghost_source():
        def act(side):
            ghost_copies(side, ["mis"])[0].start()

            @pl.when(group == last)
            def _():
                tx[side] = va[pl.ds(W, W) if side == 0 else pl.ds(X, W)]
                ghost_copies(side, ["end"])[0].start()

        both_sides(act)

    def ghost_wait(names):
        def arrived(side):
            for copy in ghost_copies(1 - side, names):
                copy.wait_recv()

        both_sides(arrived)

    def ghost_sent():
        def act(side):
            for copy in ghost_copies(side, (*DATA, "mis")):
                copy.wait_send()

            @pl.when(group == last)
            def _():
                ghost_copies(side, ["end"])[0].wait_send()

        both_sides(act)

    fine = (Z, 8, 128)

    def roots(lo, hi):
        for r in range(lo, hi):
            rootx[r] = jnp.sqrt(condx[r])

    def coefficients(r):
        k = rootx[r + 1]
        y = iota(fine, 1) * 128 + iota(fine, 2)
        zero = jnp.zeros(fine, F32)
        edge = jnp.zeros((1, 8, 128), F32)
        faces = [
            k * rootx[r],
            k * rootx[r + 2],
            jnp.where(y == 0, zero, k * y_below(k)),
            jnp.where(y == 1023, zero, k * y_above(k)),
            k * jnp.concatenate([edge, k[:-1]], 0),
            k * jnp.concatenate([k[1:], edge], 0),
        ]
        total = capx[r]
        for t in faces:
            total = total + t
        inverse = 1.0 / total
        inv[r] = inverse
        for n in range(6):
            co[n, r] = faces[n] * inverse

    def inner_coefficients():
        roots(W + 1, W + 1 + X)

        def pair(n, c):
            coefficients(W + 1 + 2 * n)
            coefficients(W + 2 + 2 * n)
            return c

        lax.fori_loop(0, (X - 2) // 2, pair, 0)

    def outer_coefficients():
        roots(0, W + 1)
        roots(W + 1 + X, NR + 2)

        def pair(n, c):
            coefficients(n)
            coefficients(W + X - 1 + n)
            return c

        lax.fori_loop(0, W + 1, pair, 0)

    outgoing(lambda copy: copy.start(), 0, HEAD)
    for copy in loads[2]:
        copy.wait()
    for k, rows in enumerate(restrict(stage[0], stage[1], stage[2])):
        crow[k] = rows
    plan_row[...] = plan_ref[...].astype(F32)

    @pl.when(swapped)
    def _():
        trade_rows().start()
        plan_copy.start()

    for copy in loads[3]:
        copy.wait()
    outgoing(lambda copy: copy.start(), HEAD)

    @pl.when(jnp.logical_not(swapped))
    def _():
        cbuf[row] = crow[...]
        gather_start()

    @pl.when(swapped)
    def _():
        pltpu.make_async_remote_copy(
            crow, cbuf.at[row], cr_s, cr_r, device_id=partner, device_id_type=MESH).wait_recv()
        gather_start()

    def outside(lo_cond, lo):
        condx[pl.ds(lo_cond, W + 1)] = jnp.zeros((W + 1, Z, 8, 128), F32)
        capx[pl.ds(lo, W)] = jnp.ones((W, Z, 8, 128), F32)
        misx[pl.ds(lo, W)] = jnp.zeros((W, Z, 8, 128), F32)
        va[pl.ds(lo, W)] = jnp.zeros((W, Z, 8, 128), F32)

    @pl.when(jnp.logical_not(has_below))
    def _():
        outside(0, 0)

    @pl.when(jnp.logical_not(has_above))
    def _():
        outside(W + 1 + X, W + X)

    @pl.when(jnp.logical_not(swapped))
    def _():
        def put(r, c):
            condx[W + 1 + r] = stage[0, r]
            capx[W + r] = stage[1, r]
            misx[W + r] = stage[3, r]
            return c

        lax.fori_loop(0, X, put, 0)
        planx[...] = plan_row[...]

        @pl.when(group == last)
        def _():
            def put_final(r, c):
                va[W + r] = stage[2, r]
                return c

            lax.fori_loop(0, X, put_final, 0)

        ghost_data()
        ghost_source()

    def gather_wait(k, c):
        gather_copy(k, (row - k + SLABS) % SLABS).wait_recv()
        return c

    lax.fori_loop(1, SLABS, gather_wait, 0)
    nothing = jnp.zeros((8, 128), F32)
    for ref in (ck, ga, gb):
        ref[0] = nothing
        ref[SLABS + 1] = nothing

    def coarse_root(r, c):
        ck[r + 1] = jnp.sqrt(cbuf[r, 0])
        return c

    lax.fori_loop(0, SLABS, coarse_root, 0)
    CH = 8
    shape = (CH, 8, 128)

    def coarse_coefficients(r):
        k = ck[pl.ds(r + 1, CH)]
        column_of = iota(shape, 2) % CY
        layer = 2 * iota(shape, 1) + iota(shape, 2) // CY
        zero = jnp.zeros(shape, F32)
        scale = float(CF * CF)
        k_below, k_above = cz_both(k)
        faces = [
            k * ck[pl.ds(r, CH)],
            k * ck[pl.ds(r + 2, CH)],
            jnp.where(column_of == 0, zero, k * pltpu.roll(k, 1, 2)),
            jnp.where(column_of == CY - 1, zero, k * pltpu.roll(k, 127, 2)),
            jnp.where(layer == 0, zero, scale * k * k_below),
            jnp.where(layer == Z - 1, zero, scale * k * k_above),
        ]
        store = cbuf[pl.ds(r, CH), 1] * float(CF * CF // STEPS)
        total = store
        for t in faces:
            total = total + t
        inverse = 1.0 / total
        for n in range(6):
            cco[n, pl.ds(r, CH)] = faces[n] * inverse
        cst[pl.ds(r, CH)] = store * inverse

    for n in range(SLABS // CH):
        coarse_coefficients(n * CH)

    def coarse_sweep(src, dst):
        for n in range(SLABS // CH):
            r = n * CH
            v = src[pl.ds(r + 1, CH)]
            c = pl.ds(r, CH)
            v_below, v_above = cz_both(v)
            new = gbi[c] + cco[0, c] * src[pl.ds(r, CH)] + cco[1, c] * src[pl.ds(r + 2, CH)]
            new = new + (cco[2, c] * pltpu.roll(v, 1, 2) + cco[3, c] * pltpu.roll(v, 127, 2))
            dst[pl.ds(r + 1, CH)] = new + (cco[4, c] * v_below + cco[5, c] * v_above)

    def coarse_step():
        gbi[...] = cst[...] * ga[pl.ds(1, SLABS)]

        def pair(n, c):
            coarse_sweep(ga, gb)
            coarse_sweep(gb, ga)
            return c

        lax.fori_loop(0, SWEEPS // 2, pair, 0)

    @pl.when(swapped)
    def _():
        incoming_data(0)
        ghost_data()

    ga[pl.ds(1, SLABS)] = cbuf[:, 2]

    def predict(n, c):
        for k in range(3):
            fore[k] = ga[row + k]
        coarse_step()
        return c

    lax.fori_loop(0, last - group + 1, predict, 0)
    adv[...] = ga[row + 1]

    def extend(rows):
        flat = jnp.concatenate([part for c8 in rows for part in (c8[:, :CY], c8[:, CY:])], axis=0)
        pick = (iota((CY, 1024), 0) == iota((CY, 1024), 1) // CF).astype(F32)
        wide = jnp.dot(flat, pick, preferred_element_type=F32, precision=EXACT)
        for s in range(8):
            for n in range(len(rows)):
                pw[n, :, s, :] = wide[Z * n:Z * (n + 1), 128 * s:128 * (s + 1)]

    def repeated(n):
        block = pw[n]
        places = [LAYERS.index(z) for z in range(Z)]
        return jnp.concatenate([block[p:p + 1] for p in places], axis=0)

    @pl.when(group < last)
    def _():
        extend([fore[0], fore[1], fore[2]])
        for part, (lo, hi) in enumerate(((0, W), (W, W + X), (W + X, NR))):
            rows = repeated(part)
            for r in range(lo, hi):
                va[r] = rows

    @pl.when(swapped)
    def _():
        incoming_data(1)

    inner_coefficients()

    @pl.when(swapped)
    def _():
        incoming_source(0)
        ghost_source()

    ghost_wait(DATA)
    outer_coefficients()

    @pl.when(swapped)
    def _():
        incoming_source(1)
        plan_copy.wait_recv()

    def sweep(src, dst, rows):
        for r in rows:
            for z in range(0, Z, 2):
                here = pl.ds(z, 2)
                v = src[r, here]
                if z == 0:
                    z_below = jnp.concatenate([v[:1], v[:1]], 0)
                else:
                    z_below = src[r, pl.ds(z - 1, 2)]
                if z == Z - 2:
                    z_above = jnp.concatenate([v[1:], v[1:]], 0)
                else:
                    z_above = src[r, pl.ds(z + 1, 2)]
                new = (bi[r, here] + co[0, r, here] * src[r - 1, here]) + co[1, r, here] * src[r + 1, here]
                new = new + (co[4, r, here] * z_below + co[5, r, here] * z_above)
                dst[r, here] = new + (co[2, r, here] * y_below(v) + co[3, r, here] * y_above(v))

    def source(lo, hi):
        rows = pl.ds(lo, hi - lo)
        bi[rows] = (capx[rows] * va[rows] + misx[rows]) * inv[rows]

    def sample():
        cell = wells_ref[...] - row * (X * Z * 1024)
        line = cell >> 7

        def part(n, c):
            v = va[pl.ds(W + 2 * n, 2)].reshape(256, 128)
            high = v.astype(BF16)
            low = (v - high.astype(F32)).astype(BF16)
            pieces = jnp.concatenate([high, low], axis=1)
            hot = jnp.where(iota((256, 1024), 0) + 256 * n == line, 1.0, 0.0).astype(BF16)
            acc[...] += lax.dot_general(pieces, hot, (((0,), (0,)), ((), ())), preferred_element_type=F32)
            return c

        acc[...] = jnp.zeros(acc.shape, F32)
        lax.fori_loop(0, X // 2, part, 0)
        lines = acc[pl.ds(0, 128)] + acc[pl.ds(128, 128)]
        mine = jnp.where(iota((128, 1024), 0) == (cell & 127), lines, 0.0)
        sums[...] += jnp.sum(mine, axis=0, keepdims=True)

    def exchange_copy(n, side):
        return pltpu.make_async_remote_copy(
            tx.at[side], rx.at[n, 1 - side], ex_s.at[n, side], ex_r.at[n, 1 - side],
            device_id=below if side == 0 else above, device_id_type=MESH)

    sums[...] = jnp.zeros(sums.shape, F32)
    per_step = SWEEPS // W
    blocks = STEPS * per_step

    def block(n, c):
        opens = n % per_step == 0

        @pl.when(opens)
        def _():
            source(W + 1, W + X - 1)

        for k in range(1, W + 1):
            src, dst = (va, vb) if k % 2 else (vb, va)
            sweep(src, dst, range(W + k, W + X - k))

        @pl.when(n == 0)
        def _():
            ghost_wait(["mis"])

            @pl.when(group == last)
            def _():
                ghost_wait(["end"])

            ghost_sent()

        @pl.when(n > 0)
        def _():
            def arrive(side):
                exchange_copy(n - 1, 1 - side).wait_recv()
                va[pl.ds(0, W) if side == 0 else pl.ds(W + X, W)] = rx[n - 1, side]
                exchange_copy(n - 1, side).wait_send()

            both_sides(arrive)

        @pl.when(opens)
        def _():
            source(0, W + 1)
            source(W + X - 1, NR)

        for k in range(1, W + 1):
            src, dst = (va, vb) if k % 2 else (vb, va)
            sweep(src, dst, [*range(k, W + k), *range(W + X - k, NR - k)])

        @pl.when(n < blocks - 1)
        def _():
            tx[0] = va[pl.ds(W, W)]
            tx[1] = va[pl.ds(X, W)]
            both_sides(lambda side: exchange_copy(n, side).start())

        @pl.when((n % per_step == per_step - 1) & (n < blocks - 1))
        def _():
            sample()

        return c

    lax.fori_loop(0, blocks, block, 0)

    st1[group] = restrict(va[body])[0] - adv[...]

    def group_copy(ref, send, receive, k, who):
        return pltpu.make_async_remote_copy(
            ref.at[who], ref.at[who], send.at[k], receive.at[k],
            device_id=device_of((group + k) % GROUPS, row), device_id_type=MESH)

    def group_start(*how):
        for k in range(1, GROUPS):
            group_copy(*how, k, group).start()

    def group_wait(*how):
        for k in range(1, GROUPS):
            group_copy(*how, k, (group - k + GROUPS) % GROUPS).wait_recv()

    group_start(st1, e1_s, e1_r)
    own_copy = pltpu.make_async_remote_copy(
        va.at[body], own, own_s, own_r, device_id=partner, device_id_type=MESH)
    @pl.when(swapped)
    def _():
        own_copy.start()

    sample()
    tot[...] = sums[...] * planx[...]
    for j in range(8):
        st2[row, 3, j:j + 1, :] = tot[:, 128 * j:128 * (j + 1)]
    group_wait(st1, e1_s, e1_r)
    for g in range(1, GROUPS):
        st2[row, g - 1] = st1[g]

    def row_copy(k, who):
        return pltpu.make_async_remote_copy(
            st2.at[who], st2.at[who], e2_s.at[k], e2_r.at[k],
            device_id=device_of(group, (row + k) % SLABS), device_id_type=MESH)

    def row_start(k, c):
        row_copy(k, row).start()
        return c

    def row_wait(k, c):
        row_copy(k, (row - k + SLABS) % SLABS).wait_recv()
        return c

    lax.fori_loop(1, SLABS, row_start, 0)
    lax.fori_loop(1, SLABS, row_wait, 0)
    st3[group] = jnp.sum(st2[:, 3], axis=0)
    group_start(st3, e3_s, e3_r)

    ga[pl.ds(1, SLABS)] = st2[:, 2]
    chain = last - period

    def correct(n, c):
        coarse_step()

        @pl.when(n < chain - 1)
        def _():
            ga[pl.ds(1, SLABS)] = ga[pl.ds(1, SLABS)] + st2[:, 1 - n]

        return c

    lax.fori_loop(0, chain, correct, 0)
    carried = jnp.where(chain > 0, 1.0, 0.0) * ga[slab + 1]
    extend([carried])
    wide = repeated(0)

    @pl.when(swapped)
    def _():
        own_copy.wait()
        for r in range(X):
            vb[W + r] = own[r] + wide

    @pl.when(jnp.logical_not(swapped))
    def _():
        for r in range(X):
            vb[W + r] = va[W + r] + wide

    outs = [
        pltpu.make_async_copy(vb.at[body, :, j, :], out_hbm.at[:, :, pl.ds(128 * j, 128)], out_sem.at[j])
        for j in range(8)
    ]
    for copy in outs:
        copy.start()
    group_wait(st3, e3_s, e3_r)
    grad_ref[...] = ((st3[0] + st3[1]) + (st3[2] + st3[3])) * (1.0 / (STEPS * GROUPS))

    def rows_sent(k, c):
        gather_copy(k, row).wait_send()
        row_copy(k, row).wait_send()
        return c

    lax.fori_loop(1, SLABS, rows_sent, 0)
    for k in range(1, GROUPS):
        group_copy(st1, e1_s, e1_r, k, group).wait_send()
        group_copy(st3, e3_s, e3_r, k, group).wait_send()
    outgoing(lambda copy: copy.wait_send())

    @pl.when(swapped)
    def _():
        trade_rows().wait_send()
        plan_copy.wait_send()

    for copy in outs:
        copy.wait()


def shards(final_level, misfit, conductivity, capacity, wells, plan):
    field = lambda *lead: pltpu.VMEM(lead + (Z, 8, 128), F32)
    tile = lambda *lead: pltpu.VMEM(lead + (8, 128), F32)
    dma = lambda *shape: pltpu.SemaphoreType.DMA(shape)
    vmem = pl.BlockSpec(memory_space=pltpu.VMEM)
    hbm = pl.BlockSpec(memory_space=pl.ANY)
    corrected, grad = pl.pallas_call(
        kernel,
        out_shape=(
            jax.ShapeDtypeStruct((X, Z, 1024), F32),
            jax.ShapeDtypeStruct((8, 128), F32),
        ),
        in_specs=[hbm, hbm, hbm, hbm, vmem, vmem],
        out_specs=(hbm, vmem),
        scratch_shapes=[
            field(4, X), field(NR + 2), field(NR), field(NR), field(NR), field(NR), field(6, NR), field(NR), field(NR),
            field(X), field(2, W), field(NEX, 2, W),
            tile(SLABS, 3), tile(3), tile(SLABS + 2), tile(6, SLABS), tile(SLABS),
            tile(SLABS + 2), tile(SLABS + 2), tile(SLABS), tile(3 * Z), field(3), tile(3), tile(),
            pltpu.VMEM((1, 1024), F32), pltpu.VMEM((1, 1024), F32), field(NR + 2), pltpu.VMEM((256, 1024), F32), pltpu.VMEM((1, 1024), F32),
            pltpu.VMEM((1, 1024), F32), tile(GROUPS), tile(SLABS, 4), tile(GROUPS),
            dma(4, 8), pltpu.SemaphoreType.DMA, pltpu.SemaphoreType.DMA, dma(SLABS), dma(SLABS),
            dma(14), dma(14), dma(2, 4), dma(2, 4), dma(NEX, 2), dma(NEX, 2),
            dma(GROUPS), dma(GROUPS), dma(SLABS), dma(SLABS), dma(GROUPS), dma(GROUPS),
            pltpu.SemaphoreType.DMA, pltpu.SemaphoreType.DMA, dma(8),
        ],
        compiler_params=pltpu.CompilerParams(
            collective_id=0, has_side_effects=True, vmem_limit_bytes=60 * 2**20
        ),
    )(
        final_level, misfit[0], conductivity, capacity,
        wells.reshape(1, -1), plan,
    )
    return corrected[None], grad.reshape(-1)


def solution(mesh):
    return jax.shard_map(
        shards,
        mesh=mesh,
        in_specs=(
            P("slab", None, None),
            P("period", "slab", None, None),
            P("slab", None, None),
            P("slab", None, None),
            P(),
            P("period", None),
        ),
        out_specs=(P("period", "slab", None, None), P()),
        check_vma=False,
    )
```

```python
import jax
import jax.numpy as jnp
from jax import lax
from jax.experimental import pallas as pl
from jax.experimental.pallas import tpu as pltpu
from jax.sharding import PartitionSpec as P

MESH = pl.DeviceIdType.MESH
F32 = jnp.float32
BF16 = jnp.bfloat16
STEPS = 2
SWEEPS = 8
CF = 16
X = 16
Z = 16
SLABS = 32
GROUPS = 4
W = 4
NR = X + 2 * W
NEX = STEPS * SWEEPS // W - 1
CY = 64
EXACT = lax.Precision.HIGHEST


def iota(shape, dim):
    return lax.broadcasted_iota(jnp.int32, shape, dim)


def y_below(v):
    rolled = pltpu.roll(v, 1, 2)
    return jnp.where(iota(v.shape, 2) == 0, pltpu.roll(rolled, 1, 1), rolled)


def y_above(v):
    rolled = pltpu.roll(v, 127, 2)
    return jnp.where(iota(v.shape, 2) == 127, pltpu.roll(rolled, 7, 1), rolled)


LAYERS = [z for h in range(2) for z in range(h, Z, 2)]


def cz_both(v):
    turned = pltpu.roll(v, 64, 2)
    upper = iota(v.shape, 2) >= 64
    below = jnp.where(upper, turned, pltpu.roll(turned, 1, 1))
    above = jnp.where(upper, pltpu.roll(turned, 7, 1), turned)
    return below, above


def device_of(group, row):
    return (2 * (group // 2) + row % 2, 2 * (row // 2) + group % 2)


def kernel(
    final_hbm, misfit_hbm, cond_hbm, cap_hbm, wells_ref, plan_ref,
    out_hbm, grad_ref,
    stage, condx, capx, misx, va, vb, co, inv, bi, own, tx, rx,
    cbuf, crow, ck, cco, cst, ga, gb, gbi, rs, pw, fore, adv, plan_row, planx, rootx, acc, sums, tot, st1, st2, st3,
    ld_sem, cr_s, cr_r, ag_s, ag_r, sw_s, sw_r, hs_s, hs_r, ex_s, ex_r, e1_s, e1_r, e2_s, e2_r, e3_s, e3_r,
    own_s, own_r, out_sem,
):
    period = lax.axis_index("period")
    slab = lax.axis_index("slab")
    x_hi, core = period // 2, period % 2
    column, x_lo = slab // 2, slab % 2
    group = 2 * x_hi + x_lo
    row = 2 * column + core
    swapped = core != x_lo
    partner = (2 * x_hi + 1 - core, 2 * column + 1 - x_lo)
    far = (2 * (1 - x_hi) + core, 2 * column + 1 - x_lo)
    last = GROUPS - 1

    def load(k):
        src = (cond_hbm, cap_hbm, final_hbm, misfit_hbm)[k]
        return [
            pltpu.make_async_copy(src.at[:, :, pl.ds(128 * j, 128)], stage.at[k, :, :, j, :], ld_sem.at[k, j])
            for j in range(8)
        ]

    loads = [load(k) for k in range(4)]
    for group_of in loads:
        for copy in group_of:
            copy.start()

    barrier = pltpu.get_barrier_semaphore()

    def hello(device):
        pl.semaphore_signal(barrier, inc=1, device_id=device, device_id_type=MESH)

    def greet(k, c):
        hello(device_of(group, (row + k) % SLABS))
        return c

    lax.fori_loop(1, SLABS, greet, 0)
    for k in range(1, GROUPS):
        hello(device_of((group + k) % GROUPS, row))

    @pl.when(swapped)
    def _():
        hello(partner)

    def restrict(*blocks):
        for n, block in enumerate(blocks):
            summed = jnp.sum(block, axis=0)
            rs[pl.ds(Z * n, Z)] = jnp.concatenate([summed[z:z + 1] for z in LAYERS], axis=0)
        rows = Z * len(blocks)
        flat = jnp.concatenate([rs[pl.ds(0, rows), s, :] for s in range(8)], axis=1)
        pick = (iota((1024, CY), 1) == iota((1024, CY), 0) // CF).astype(F32)
        total = jnp.dot(flat, pick, preferred_element_type=F32, precision=EXACT) * (1.0 / (CF * CF))
        return [
            jnp.concatenate([total[Z * n:Z * n + 8], total[Z * n + 8:Z * n + Z]], axis=1)
            for n in range(len(blocks))
        ]

    for k in (0, 1):
        for copy in loads[k]:
            copy.wait()
    pl.semaphore_wait(barrier, (SLABS - 1) + GROUPS - 1 + swapped.astype(jnp.int32))

    def trade_rows():
        return pltpu.make_async_remote_copy(
            crow, cbuf.at[2 * column + x_lo], cr_s, cr_r, device_id=partner, device_id_type=MESH)

    def gather_copy(k, who):
        return pltpu.make_async_remote_copy(
            cbuf.at[who], cbuf.at[who], ag_s.at[k], ag_r.at[k],
            device_id=device_of(group, (row + k) % SLABS), device_id_type=MESH)

    def gather_start():
        def start(k, c):
            gather_copy(k, row).start()
            return c

        lax.fori_loop(1, SLABS, start, 0)

    body = pl.ds(W, X)

    def trade(k, ref, shift, n, lo, rows, device):
        return pltpu.make_async_remote_copy(
            stage.at[k, pl.ds(lo, rows)], ref.at[pl.ds(shift + lo, rows)], sw_s.at[n], sw_r.at[n],
            device_id=device, device_id_type=MESH)

    def trade_mis(d):
        return [trade(3, misx, W, 0, 0, W, d), trade(3, misx, W, 1, X - W, W, d)], [trade(3, misx, W, 2, W, X - 2 * W, d)]

    def trade_cap(d):
        return [trade(1, capx, W, 3, 0, W, d), trade(1, capx, W, 4, X - W, W, d)], [trade(1, capx, W, 5, W, X - 2 * W, d)]

    def trade_low(d):
        return [trade(0, condx, W + 1, 6, 0, W + 1, d)], [trade(0, condx, W + 1, 7, W + 1, X // 2 - W - 1, d)]

    def trade_high(d):
        return [trade(0, condx, W + 1, 8, X - W - 1, W + 1, d)], [trade(0, condx, W + 1, 9, X // 2, X // 2 - W - 1, d)]

    def trade_end(d):
        return [trade(2, va, W, 10, 0, W, d), trade(2, va, W, 11, X - W, W, d)], [trade(2, va, W, 12, W, X - 2 * W, d)]

    plan_copy = pltpu.make_async_remote_copy(
        plan_row, planx, sw_s.at[13], sw_r.at[13], device_id=partner, device_id_type=MESH)
    to_last = (x_hi == 1) & (x_lo == 0)
    far_last = (x_hi == 0) & (x_lo == 0)

    def in_order(*lists):
        return [copy for pairs in lists for part in range(2) for pair in pairs for copy in pair[part]]

    HEAD = 2

    def outgoing(act, lo=0, hi=None):
        @pl.when(swapped & to_last)
        def _():
            for copy in in_order([trade_cap(partner)], [trade_mis(partner)])[lo:hi]:
                act(copy)

        @pl.when(swapped & jnp.logical_not(to_last))
        def _():
            for copy in in_order([trade_low(partner)], [trade_mis(partner)])[lo:hi]:
                act(copy)

        @pl.when(jnp.logical_not(swapped) & far_last)
        def _():
            for copy in in_order([trade_low(far), trade_high(far)], [trade_end(far)])[lo:hi]:
                act(copy)

        @pl.when(jnp.logical_not(swapped) & jnp.logical_not(far_last))
        def _():
            for copy in in_order([trade_cap(far), trade_high(far)])[lo:hi]:
                act(copy)

    def incoming_data(part):
        for pair in (trade_cap(far), trade_high(far), trade_low(far)):
            for copy in pair[part]:
                copy.wait_recv()

    def incoming_source(part):
        for copy in trade_mis(partner)[part]:
            copy.wait_recv()

        @pl.when(group == last)
        def _():
            for copy in trade_end(partner)[part]:
                copy.wait_recv()

    below = device_of(group, (row + SLABS - 1) % SLABS)
    above = device_of(group, (row + 1) % SLABS)
    has_below = row > 0
    has_above = row < SLABS - 1

    def ghost_copies(side, names):
        device = below if side == 0 else above
        cut, put = (pl.ds(W, W), pl.ds(W + X, W)) if side == 0 else (pl.ds(X, W), pl.ds(0, W))
        wide_cut, wide_put = (
            (pl.ds(W + 1, W + 1), pl.ds(W + 1 + X, W + 1)) if side == 0 else (pl.ds(X, W + 1), pl.ds(0, W + 1)))
        table = {
            "cond": (0, condx.at[wide_cut], condx.at[wide_put]),
            "cap": (1, capx.at[cut], capx.at[put]),
            "mis": (2, misx.at[cut], misx.at[put]),
            "end": (3, tx.at[side], va.at[put]),
        }
        return [
            pltpu.make_async_remote_copy(
                table[name][1], table[name][2], hs_s.at[side, table[name][0]], hs_r.at[side, table[name][0]],
                device_id=device, device_id_type=MESH)
            for name in names
        ]

    def both_sides(act):
        @pl.when(has_below)
        def _():
            act(0)

        @pl.when(has_above)
        def _():
            act(1)

    DATA = ("cond", "cap")

    def ghost_data():
        def act(side):
            for copy in ghost_copies(side, DATA):
                copy.start()

        both_sides(act)

    def ghost_source():
        def act(side):
            ghost_copies(side, ["mis"])[0].start()

            @pl.when(group == last)
            def _():
                tx[side] = va[pl.ds(W, W) if side == 0 else pl.ds(X, W)]
                ghost_copies(side, ["end"])[0].start()

        both_sides(act)

    def ghost_wait(names):
        def arrived(side):
            for copy in ghost_copies(1 - side, names):
                copy.wait_recv()

        both_sides(arrived)

    def ghost_sent():
        def act(side):
            for copy in ghost_copies(side, (*DATA, "mis")):
                copy.wait_send()

            @pl.when(group == last)
            def _():
                ghost_copies(side, ["end"])[0].wait_send()

        both_sides(act)

    fine = (Z, 8, 128)

    def roots(lo, hi):
        for r in range(lo, hi):
            rootx[r] = jnp.sqrt(condx[r])

    def coefficients(r):
        k = rootx[r + 1]
        y = iota(fine, 1) * 128 + iota(fine, 2)
        zero = jnp.zeros(fine, F32)
        edge = jnp.zeros((1, 8, 128), F32)
        faces = [
            k * rootx[r],
            k * rootx[r + 2],
            jnp.where(y == 0, zero, k * y_below(k)),
            jnp.where(y == 1023, zero, k * y_above(k)),
            k * jnp.concatenate([edge, k[:-1]], 0),
            k * jnp.concatenate([k[1:], edge], 0),
        ]
        total = capx[r]
        for t in faces:
            total = total + t
        inverse = 1.0 / total
        inv[r] = inverse
        for n in range(6):
            co[n, r] = faces[n] * inverse

    def inner_coefficients():
        roots(W + 1, W + 1 + X)

        def pair(n, c):
            coefficients(W + 1 + 2 * n)
            coefficients(W + 2 + 2 * n)
            return c

        lax.fori_loop(0, (X - 2) // 2, pair, 0)

    def outer_coefficients():
        roots(0, W + 1)
        roots(W + 1 + X, NR + 2)

        def pair(n, c):
            coefficients(n)
            coefficients(W + X - 1 + n)
            return c

        lax.fori_loop(0, W + 1, pair, 0)

    outgoing(lambda copy: copy.start(), 0, HEAD)
    for copy in loads[2]:
        copy.wait()
    for k, rows in enumerate(restrict(stage[0], stage[1], stage[2])):
        crow[k] = rows
    plan_row[...] = plan_ref[...].astype(F32)

    @pl.when(swapped)
    def _():
        trade_rows().start()
        plan_copy.start()

    for copy in loads[3]:
        copy.wait()
    outgoing(lambda copy: copy.start(), HEAD)

    @pl.when(jnp.logical_not(swapped))
    def _():
        cbuf[row] = crow[...]
        gather_start()

    @pl.when(swapped)
    def _():
        pltpu.make_async_remote_copy(
            crow, cbuf.at[row], cr_s, cr_r, device_id=partner, device_id_type=MESH).wait_recv()
        gather_start()

    def outside(lo_cond, lo):
        condx[pl.ds(lo_cond, W + 1)] = jnp.zeros((W + 1, Z, 8, 128), F32)
        capx[pl.ds(lo, W)] = jnp.ones((W, Z, 8, 128), F32)
        misx[pl.ds(lo, W)] = jnp.zeros((W, Z, 8, 128), F32)
        va[pl.ds(lo, W)] = jnp.zeros((W, Z, 8, 128), F32)

    @pl.when(jnp.logical_not(has_below))
    def _():
        outside(0, 0)

    @pl.when(jnp.logical_not(has_above))
    def _():
        outside(W + 1 + X, W + X)

    @pl.when(jnp.logical_not(swapped))
    def _():
        def put(r, c):
            condx[W + 1 + r] = stage[0, r]
            capx[W + r] = stage[1, r]
            misx[W + r] = stage[3, r]
            return c

        lax.fori_loop(0, X, put, 0)
        planx[...] = plan_row[...]

        @pl.when(group == last)
        def _():
            def put_final(r, c):
                va[W + r] = stage[2, r]
                return c

            lax.fori_loop(0, X, put_final, 0)

        ghost_data()
        ghost_source()

    def gather_wait(k, c):
        gather_copy(k, (row - k + SLABS) % SLABS).wait_recv()
        return c

    lax.fori_loop(1, SLABS, gather_wait, 0)
    nothing = jnp.zeros((8, 128), F32)
    for ref in (ck, ga, gb):
        ref[0] = nothing
        ref[SLABS + 1] = nothing

    def coarse_root(r, c):
        ck[r + 1] = jnp.sqrt(cbuf[r, 0])
        return c

    lax.fori_loop(0, SLABS, coarse_root, 0)
    CH = 8
    shape = (CH, 8, 128)

    def coarse_coefficients(r):
        k = ck[pl.ds(r + 1, CH)]
        column_of = iota(shape, 2) % CY
        layer = 2 * iota(shape, 1) + iota(shape, 2) // CY
        zero = jnp.zeros(shape, F32)
        scale = float(CF * CF)
        k_below, k_above = cz_both(k)
        faces = [
            k * ck[pl.ds(r, CH)],
            k * ck[pl.ds(r + 2, CH)],
            jnp.where(column_of == 0, zero, k * pltpu.roll(k, 1, 2)),
            jnp.where(column_of == CY - 1, zero, k * pltpu.roll(k, 127, 2)),
            jnp.where(layer == 0, zero, scale * k * k_below),
            jnp.where(layer == Z - 1, zero, scale * k * k_above),
        ]
        store = cbuf[pl.ds(r, CH), 1] * float(CF * CF // STEPS)
        total = store
        for t in faces:
            total = total + t
        inverse = 1.0 / total
        for n in range(6):
            cco[n, pl.ds(r, CH)] = faces[n] * inverse
        cst[pl.ds(r, CH)] = store * inverse

    for n in range(SLABS // CH):
        coarse_coefficients(n * CH)

    def coarse_sweep(src, dst):
        for n in range(SLABS // CH):
            r = n * CH
            v = src[pl.ds(r + 1, CH)]
            c = pl.ds(r, CH)
            v_below, v_above = cz_both(v)
            new = gbi[c] + cco[0, c] * src[pl.ds(r, CH)] + cco[1, c] * src[pl.ds(r + 2, CH)]
            new = new + (cco[2, c] * pltpu.roll(v, 1, 2) + cco[3, c] * pltpu.roll(v, 127, 2))
            dst[pl.ds(r + 1, CH)] = new + (cco[4, c] * v_below + cco[5, c] * v_above)

    def coarse_step():
        gbi[...] = cst[...] * ga[pl.ds(1, SLABS)]

        def pair(n, c):
            coarse_sweep(ga, gb)
            coarse_sweep(gb, ga)
            return c

        lax.fori_loop(0, SWEEPS // 2, pair, 0)

    @pl.when(swapped)
    def _():
        incoming_data(0)
        ghost_data()

    ga[pl.ds(1, SLABS)] = cbuf[:, 2]

    def predict(n, c):
        for k in range(3):
            fore[k] = ga[row + k]
        coarse_step()
        return c

    lax.fori_loop(0, last - group + 1, predict, 0)
    adv[...] = ga[row + 1]

    def extend(rows):
        flat = jnp.concatenate([part for c8 in rows for part in (c8[:, :CY], c8[:, CY:])], axis=0)
        pick = (iota((CY, 1024), 0) == iota((CY, 1024), 1) // CF).astype(F32)
        wide = jnp.dot(flat, pick, preferred_element_type=F32, precision=EXACT)
        for s in range(8):
            for n in range(len(rows)):
                pw[n, :, s, :] = wide[Z * n:Z * (n + 1), 128 * s:128 * (s + 1)]

    def repeated(n):
        block = pw[n]
        places = [LAYERS.index(z) for z in range(Z)]
        return jnp.concatenate([block[p:p + 1] for p in places], axis=0)

    @pl.when(group < last)
    def _():
        extend([fore[0], fore[1], fore[2]])
        for part, (lo, hi) in enumerate(((0, W), (W, W + X), (W + X, NR))):
            rows = repeated(part)
            for r in range(lo, hi):
                va[r] = rows

    @pl.when(swapped)
    def _():
        incoming_data(1)

    inner_coefficients()

    @pl.when(swapped)
    def _():
        incoming_source(0)
        ghost_source()

    ghost_wait(DATA)
    outer_coefficients()

    @pl.when(swapped)
    def _():
        incoming_source(1)
        plan_copy.wait_recv()

    def sweep(src, dst, rows):
        for r in rows:
            for z in range(0, Z, 2):
                here = pl.ds(z, 2)
                v = src[r, here]
                if z == 0:
                    z_below = jnp.concatenate([v[:1], v[:1]], 0)
                else:
                    z_below = src[r, pl.ds(z - 1, 2)]
                if z == Z - 2:
                    z_above = jnp.concatenate([v[1:], v[1:]], 0)
                else:
                    z_above = src[r, pl.ds(z + 1, 2)]
                new = (bi[r, here] + co[0, r, here] * src[r - 1, here]) + co[1, r, here] * src[r + 1, here]
                new = new + (co[4, r, here] * z_below + co[5, r, here] * z_above)
                dst[r, here] = new + (co[2, r, here] * y_below(v) + co[3, r, here] * y_above(v))

    def source(lo, hi):
        rows = pl.ds(lo, hi - lo)
        bi[rows] = (capx[rows] * va[rows] + misx[rows]) * inv[rows]

    def sample():
        cell = wells_ref[...] - row * (X * Z * 1024)
        line = cell >> 7

        def part(n, c):
            v = va[pl.ds(W + 2 * n, 2)].reshape(256, 128)
            high = v.astype(BF16)
            low = (v - high.astype(F32)).astype(BF16)
            pieces = jnp.concatenate([high, low], axis=1)
            hot = jnp.where(iota((256, 1024), 0) + 256 * n == line, 1.0, 0.0).astype(BF16)
            acc[...] += lax.dot_general(pieces, hot, (((0,), (0,)), ((), ())), preferred_element_type=F32)
            return c

        acc[...] = jnp.zeros(acc.shape, F32)
        lax.fori_loop(0, X // 2, part, 0)
        lines = acc[pl.ds(0, 128)] + acc[pl.ds(128, 128)]
        mine = jnp.where(iota((128, 1024), 0) == (cell & 127), lines, 0.0)
        sums[...] += jnp.sum(mine, axis=0, keepdims=True)

    def exchange_copy(n, side):
        return pltpu.make_async_remote_copy(
            tx.at[side], rx.at[n, 1 - side], ex_s.at[n, side], ex_r.at[n, 1 - side],
            device_id=below if side == 0 else above, device_id_type=MESH)

    sums[...] = jnp.zeros(sums.shape, F32)
    per_step = SWEEPS // W
    blocks = STEPS * per_step

    def block(n, c):
        opens = n % per_step == 0

        @pl.when(opens)
        def _():
            source(W + 1, W + X - 1)

        for k in range(1, W + 1):
            src, dst = (va, vb) if k % 2 else (vb, va)
            sweep(src, dst, range(W + k, W + X - k))

        @pl.when(n == 0)
        def _():
            ghost_wait(["mis"])

            @pl.when(group == last)
            def _():
                ghost_wait(["end"])

            ghost_sent()

        def outer(side):
            has = has_below if side == 0 else has_above
            put = pl.ds(0, W) if side == 0 else pl.ds(W + X, W)

            @pl.when((n > 0) & has)
            def _():
                exchange_copy(n - 1, 1 - side).wait_recv()
                va[put] = rx[n - 1, side]
                exchange_copy(n - 1, side).wait_send()

            @pl.when(opens)
            def _():
                if side == 0:
                    source(0, W + 1)
                else:
                    source(W + X - 1, NR)

            for k in range(1, W + 1):
                src, dst = (va, vb) if k % 2 else (vb, va)
                sweep(src, dst, range(k, W + k) if side == 0 else range(W + X - k, NR - k))

            @pl.when((n < blocks - 1) & has)
            def _():
                tx[side] = va[pl.ds(W, W) if side == 0 else pl.ds(X, W)]
                exchange_copy(n, side).start()

        @pl.when(core == 0)
        def _():
            outer(1)
            outer(0)

        @pl.when(core == 1)
        def _():
            outer(0)
            outer(1)

        @pl.when((n % per_step == per_step - 1) & (n < blocks - 1))
        def _():
            sample()

        return c

    lax.fori_loop(0, blocks, block, 0)

    st1[group] = restrict(va[body])[0] - adv[...]

    def group_copy(ref, send, receive, k, who):
        return pltpu.make_async_remote_copy(
            ref.at[who], ref.at[who], send.at[k], receive.at[k],
            device_id=device_of((group + k) % GROUPS, row), device_id_type=MESH)

    def group_start(*how):
        for k in range(1, GROUPS):
            group_copy(*how, k, group).start()

    def group_wait(*how):
        for k in range(1, GROUPS):
            group_copy(*how, k, (group - k + GROUPS) % GROUPS).wait_recv()

    group_start(st1, e1_s, e1_r)
    own_copy = pltpu.make_async_remote_copy(
        va.at[body], own, own_s, own_r, device_id=partner, device_id_type=MESH)
    @pl.when(swapped)
    def _():
        own_copy.start()

    sample()
    tot[...] = sums[...] * planx[...]
    for j in range(8):
        st2[core, column, 3, j:j + 1, :] = tot[:, 128 * j:128 * (j + 1)]
    group_wait(st1, e1_s, e1_r)
    for g in range(1, GROUPS):
        st2[core, column, g - 1] = st1[g]

    CHIPS = SLABS // 2

    def chip_copy(k, who):
        return pltpu.make_async_remote_copy(
            st2.at[core, who], st2.at[core, who], e2_s.at[k], e2_r.at[k],
            device_id=device_of(group, 2 * ((column + k) % CHIPS) + core), device_id_type=MESH)

    def chip_start(k, c):
        chip_copy(k, column).start()
        return c

    def chip_wait(k, c):
        chip_copy(k, (column - k + CHIPS) % CHIPS).wait_recv()
        return c

    def pair_copy(who):
        return pltpu.make_async_remote_copy(
            st2.at[who], st2.at[who], e2_s.at[0], e2_r.at[0],
            device_id=device_of(group, 2 * column + 1 - core), device_id_type=MESH)

    lax.fori_loop(1, CHIPS, chip_start, 0)
    lax.fori_loop(1, CHIPS, chip_wait, 0)
    pair_copy(core).start()
    pair_copy(1 - core).wait_recv()

    def jumps(k):
        return [(2 * chip + odd, st2[odd, chip, k]) for chip in range(CHIPS) for odd in range(2)]

    st3[group] = jnp.sum(st2[0, :, 3], axis=0) + jnp.sum(st2[1, :, 3], axis=0)
    group_start(st3, e3_s, e3_r)

    for r, rows in jumps(2):
        ga[1 + r] = rows
    chain = last - period

    def correct(n, c):
        coarse_step()

        @pl.when(n < chain - 1)
        def _():
            for r, rows in jumps(1 - n):
                ga[1 + r] = ga[1 + r] + rows

        return c

    lax.fori_loop(0, chain, correct, 0)
    carried = jnp.where(chain > 0, 1.0, 0.0) * ga[slab + 1]
    extend([carried])
    wide = repeated(0)

    @pl.when(swapped)
    def _():
        own_copy.wait()
        for r in range(X):
            vb[W + r] = own[r] + wide

    @pl.when(jnp.logical_not(swapped))
    def _():
        for r in range(X):
            vb[W + r] = va[W + r] + wide

    outs = [
        pltpu.make_async_copy(vb.at[body, :, j, :], out_hbm.at[:, :, pl.ds(128 * j, 128)], out_sem.at[j])
        for j in range(8)
    ]
    for copy in outs:
        copy.start()
    group_wait(st3, e3_s, e3_r)
    grad_ref[...] = ((st3[0] + st3[1]) + (st3[2] + st3[3])) * (1.0 / (STEPS * GROUPS))

    def rows_sent(k, c):
        gather_copy(k, row).wait_send()
        return c

    def chips_sent(k, c):
        chip_copy(k, column).wait_send()
        return c

    lax.fori_loop(1, SLABS, rows_sent, 0)
    lax.fori_loop(1, CHIPS, chips_sent, 0)
    pair_copy(core).wait_send()
    for k in range(1, GROUPS):
        group_copy(st1, e1_s, e1_r, k, group).wait_send()
        group_copy(st3, e3_s, e3_r, k, group).wait_send()
    outgoing(lambda copy: copy.wait_send())

    @pl.when(swapped)
    def _():
        trade_rows().wait_send()
        plan_copy.wait_send()

    for copy in outs:
        copy.wait()


def shards(final_level, misfit, conductivity, capacity, wells, plan):
    field = lambda *lead: pltpu.VMEM(lead + (Z, 8, 128), F32)
    tile = lambda *lead: pltpu.VMEM(lead + (8, 128), F32)
    dma = lambda *shape: pltpu.SemaphoreType.DMA(shape)
    vmem = pl.BlockSpec(memory_space=pltpu.VMEM)
    hbm = pl.BlockSpec(memory_space=pl.ANY)
    corrected, grad = pl.pallas_call(
        kernel,
        out_shape=(
            jax.ShapeDtypeStruct((X, Z, 1024), F32),
            jax.ShapeDtypeStruct((8, 128), F32),
        ),
        in_specs=[hbm, hbm, hbm, hbm, vmem, vmem],
        out_specs=(hbm, vmem),
        scratch_shapes=[
            field(4, X), field(NR + 2), field(NR), field(NR), field(NR), field(NR), field(6, NR), field(NR), field(NR),
            field(X), field(2, W), field(NEX, 2, W),
            tile(SLABS, 3), tile(3), tile(SLABS + 2), tile(6, SLABS), tile(SLABS),
            tile(SLABS + 2), tile(SLABS + 2), tile(SLABS), tile(3 * Z), field(3), tile(3), tile(),
            pltpu.VMEM((1, 1024), F32), pltpu.VMEM((1, 1024), F32), field(NR + 2), pltpu.VMEM((256, 1024), F32), pltpu.VMEM((1, 1024), F32),
            pltpu.VMEM((1, 1024), F32), tile(GROUPS), tile(2, SLABS // 2, 4), tile(GROUPS),
            dma(4, 8), pltpu.SemaphoreType.DMA, pltpu.SemaphoreType.DMA, dma(SLABS), dma(SLABS),
            dma(14), dma(14), dma(2, 4), dma(2, 4), dma(NEX, 2), dma(NEX, 2),
            dma(GROUPS), dma(GROUPS), dma(SLABS), dma(SLABS), dma(GROUPS), dma(GROUPS),
            pltpu.SemaphoreType.DMA, pltpu.SemaphoreType.DMA, dma(8),
        ],
        compiler_params=pltpu.CompilerParams(
            collective_id=0, has_side_effects=True, vmem_limit_bytes=60 * 2**20
        ),
    )(
        final_level, misfit[0], conductivity, capacity,
        wells.reshape(1, -1), plan,
    )
    return corrected[None], grad.reshape(-1)


def solution(mesh):
    return jax.shard_map(
        shards,
        mesh=mesh,
        in_specs=(
            P("slab", None, None),
            P("period", "slab", None, None),
            P("slab", None, None),
            P("slab", None, None),
            P(),
            P("period", None),
        ),
        out_specs=(P("period", "slab", None, None), P()),
        check_vma=False,
    )
```
